32 devices in a mesh: dp: 8 (over z, core), bal: 4 (over y, x).
Axes of the slice: x: 2, y: 2, z: 4, core: 2. Of those that a mesh axis runs over, the one named last changes fastest.
Arguments:
- tiles: bfloat16 [736, 270, 256], P(('dp', 'bal')), may hold values from -6 to 6
- cotangent: bfloat16 [736, 32, 256], P(('dp', 'bal')), may hold values from -6 to 6
- halo_flags: int32 [736, 3], P(('dp', 'bal')), may hold values 0 or 1
- send_plan: int32 [32, 4, 6], P(('dp', 'bal')), may hold values from -1 to 22, as said below
- spatial_weight: bfloat16 [2304, 256], P('bal'), may hold values from -0.125 to 0.125
- temporal_weight: bfloat16 [512, 256], P('bal'), may hold values from -0.25 to 0.25
Outputs:
- features: bfloat16 [736, 32, 256], P(('dp', 'bal'))
- spatial_grad: float32 [2304, 256], P('bal', 'dp')
- temporal_grad: float32 [512, 256], P('bal', 'dp')
The draws below stay inside these ranges and needn't reach their ends.
Inputs may be any that keep to these rules, and one draw needn't show every extreme that they name: `send_plan`: row g lists, for each worker w of owner g's bal group (bal index w, same dp index) and each pair slot q, the owner's tile slot sent there, or -1. The live slots of an owner are its slots 0 to n - 1, each named exactly once, with n from 1 to 23; in every group some owner has exactly 23. One owner sends at most 6 tiles to one worker, and some pair holds exactly 6; every worker receives exactly 12 tiles.
All inputs are finite; a program needn't handle non-finite values. No bound on the sum of `halo_flags` on one device may be relied on, other than what follows from the above.
Results may differ from the reference program's by a relative error of at most 0.0049.
Values may be sent and summed in bfloat16 or wider, within the bound.
A program may use at most 128 MiB of HBM per device.

```python
import jax
import jax.numpy as jnp
from jax import lax

C = 256
TILE_ROWS = 2
TILE_COLUMNS = 4
OUTPUT_FRAMES = 4
TEMPORAL_DILATION = 2
WORK_TILES = 12
OWNED = 23
CAPACITY = 6
IN_FR = 6
IN_H = 5
IN_W = 9
IN_PIX = 270
OUT_PIX = 32
OWN_SLOTS = 736
N_DP = 8
N_BAL = 4


def group_table(key):
    key_pairs, key_owner, key_worker = jax.random.split(key, 3)
    tile_total = N_BAL * WORK_TILES
    imbalance = jax.random.randint(key_pairs, (N_BAL // 2,), 0, WORK_TILES)
    imbalance = imbalance.at[0].set(WORK_TILES - 1)
    ordered = jnp.stack([WORK_TILES + imbalance, WORK_TILES - imbalance], axis=1).reshape(N_BAL)
    owner_order = jax.random.permutation(key_owner, N_BAL)
    tile_counts = jnp.zeros((N_BAL,), jnp.int32).at[owner_order].set(ordered.astype(jnp.int32))
    range_ends = jnp.cumsum(tile_counts)
    range_starts = range_ends - tile_counts
    tile_ids = jnp.arange(tile_total, dtype=jnp.int32)
    owner_ids = jnp.sum((range_ends[None, :] <= tile_ids[:, None]).astype(jnp.int32), axis=1)
    slot_ids = tile_ids - range_starts[owner_ids]
    block_ids = tile_ids // CAPACITY
    worker_order = jax.random.permutation(key_worker, N_BAL).astype(jnp.int32)
    worker_ids = worker_order[block_ids % N_BAL]
    same_pair = (owner_ids[:, None] == owner_ids[None, :]) & (worker_ids[:, None] == worker_ids[None, :]) & (tile_ids[None, :] < tile_ids[:, None])
    pair_rank = jnp.sum(same_pair.astype(jnp.int32), axis=1)
    send_table = jnp.full((N_BAL, N_BAL, CAPACITY), -1, jnp.int32)
    return send_table.at[owner_ids, worker_ids, pair_rank].set(slot_ids)


def draw_send_plan(key, part):
    base_key = jax.random.fold_in(key, 11)
    key_list = jax.random.split(base_key, N_DP)
    tables = jax.vmap(group_table)(key_list)
    return tables.reshape(N_DP * N_BAL, N_BAL, CAPACITY)


def plant(array, key, low, top_value):
    shape = array.shape
    spot = [jax.random.randint(jax.random.fold_in(key, axis), (), 0, shape[axis]) for axis in range(len(shape))]
    array = array.at[tuple(spot)].set(low)
    longest = shape.index(max(shape))
    spot[longest] = (spot[longest] + 1) % shape[longest]
    return array.at[tuple(spot)].set(top_value)


def levels(key, shape, cuts, smallest, largest):
    level = 1.0
    for position, blocks in cuts:
        draws = jax.random.uniform(jax.random.fold_in(jax.random.fold_in(key, 6), position), (blocks,), jnp.float32, smallest / len(cuts), largest / len(cuts))
        level = level * jnp.repeat(jnp.exp(draws), shape[position] // blocks).reshape((-1,) + (1,) * (len(shape) - 1 - position))
    return level


def gaussian(key, extent, width, limit, cuts=(), held_as=jnp.bfloat16):
    entries = width * jax.random.normal(key, extent, jnp.float32)
    if cuts:
        entries = entries * levels(key, extent, cuts, -0.22, 0.18)
    return jnp.clip(entries, -limit, limit).astype(held_as)


def setup_inputs(seed: int = 0) -> dict:
    seeds = jax.random.split(jax.random.key(seed), 7)
    tiles = gaussian(seeds[0], (OWN_SLOTS, IN_PIX, C), 1.0, 6.0, ((0, 32),))
    cotangent = gaussian(seeds[1], (OWN_SLOTS, OUT_PIX, C), 1.0, 6.0, ((0, 32),))
    halo_flags = plant((jax.random.randint(seeds[2], (OWN_SLOTS, 3), 0, 2) < 1).astype(jnp.int32), jax.random.fold_in(seeds[2], 1), 0, 1)
    send_plan = draw_send_plan(jax.random.fold_in(seeds[6], 71), 0)
    spatial_weight = gaussian(seeds[4], (9 * C, C), (9 * C) ** -0.5, 0.125, ((0, 4),))
    temporal_weight = gaussian(seeds[5], (2 * C, C), (2 * C) ** -0.5, 0.25, ((0, 4),))
    return dict(tiles=tiles, cotangent=cotangent, halo_flags=halo_flags, send_plan=send_plan, spatial_weight=spatial_weight, temporal_weight=temporal_weight)


def keep_mask(halo_flag_row):
    frame_indices = jnp.arange(IN_FR)[:, None, None]
    row_ids = jnp.arange(IN_H)[None, :, None]
    col_ids = jnp.arange(IN_W)[None, None, :]
    top_ok = (row_ids > 0) | (halo_flag_row[0] > 0)
    left_ok = (col_ids > 0) | (halo_flag_row[1] > 0)
    past_frame_valid = (frame_indices >= TEMPORAL_DILATION) | (halo_flag_row[2] > 0)
    return top_ok & left_ok & past_frame_valid

def tile_pass(inputs, cotang, spatial_full, temporal_full):
    tile_number = inputs.shape[0]
    channel_index = inputs.shape[-1]
    tap_list = []
    for row_tap in range(3):
        for col_tap in range(3):
            tap_list.append(inputs[:, :, row_tap:row_tap + 2 * TILE_ROWS - 1:2, col_tap:col_tap + 2 * TILE_COLUMNS - 1:2, :])
    patches = jnp.concatenate(tap_list, axis=-1).reshape(-1, 9 * channel_index)
    pre_act = jnp.dot(patches, spatial_full, preferred_element_type=jnp.float32)
    activation = jax.nn.silu(pre_act).astype(jnp.bfloat16).reshape(tile_number, IN_FR, TILE_ROWS * TILE_COLUMNS, channel_index)
    paired_tiles = jnp.concatenate([activation[:, TEMPORAL_DILATION:], activation[:, :OUTPUT_FRAMES]], axis=-1).reshape(-1, 2 * channel_index)
    outputs = jnp.dot(paired_tiles, temporal_full, preferred_element_type=jnp.float32).astype(jnp.bfloat16)
    grad_out = cotang.reshape(-1, channel_index)
    grad_temp = lax.dot_general(paired_tiles, grad_out, (((0,), (0,)), ((), ())), preferred_element_type=jnp.float32)
    grad_pair = lax.dot_general(grad_out, temporal_full, (((1,), (1,)), ((), ())), preferred_element_type=jnp.float32)
    grad_pair = grad_pair.reshape(tile_number, OUTPUT_FRAMES, TILE_ROWS * TILE_COLUMNS, 2 * channel_index)
    causal_padding = jnp.zeros((tile_number, TEMPORAL_DILATION, TILE_ROWS * TILE_COLUMNS, channel_index), jnp.float32)
    grad_activ = jnp.concatenate([causal_padding, grad_pair[..., :channel_index]], axis=1) + jnp.concatenate([grad_pair[..., channel_index:], causal_padding], axis=1)
    pre_view = pre_act.reshape(grad_activ.shape)
    sigmoid_v = jax.nn.sigmoid(pre_view)
    grad_pre = (grad_activ * sigmoid_v * (1.0 + pre_view * (1.0 - sigmoid_v))).astype(jnp.bfloat16).reshape(-1, channel_index)
    grad_space = lax.dot_general(patches, grad_pre, (((0,), (0,)), ((), ())), preferred_element_type=jnp.float32)
    return (outputs.reshape(tile_number, OUT_PIX, channel_index), grad_space, grad_temp)

def reference(tiles, cotangent, halo_flags, send_plan, spatial_weight, temporal_weight):
    device_count = N_DP * N_BAL
    slot_ids = jnp.arange(OWNED, dtype=jnp.int32)
    plan_rows = send_plan.reshape(device_count, N_BAL * CAPACITY)
    live_all = jnp.any(plan_rows[:, :, None] == slot_ids[None, None, :], axis=1).reshape(-1)
    tile_view = tiles.reshape(OWN_SLOTS, IN_FR, IN_H, IN_W, C)
    cot_view = cotangent.reshape(OWN_SLOTS, OUTPUT_FRAMES, TILE_ROWS, TILE_COLUMNS, C)

    def one_tile(carry, item):
        tile_one, cot_one, flag_one, live_one = item

        def run_tile(sums):
            masked = jnp.where(keep_mask(flag_one)[..., None], tile_one, jnp.zeros_like(tile_one))
            outputs, grad_space, grad_temp = tile_pass(masked[None], cot_one[None], spatial_weight, temporal_weight)
            return (outputs[0], sums[0] + grad_space, sums[1] + grad_temp)

        def skip_tile(sums):
            return (jnp.zeros((OUT_PIX, C), jnp.bfloat16), sums[0], sums[1])
        outputs, sum_space, sum_temp = lax.cond(live_one, run_tile, skip_tile, carry)
        return ((sum_space, sum_temp), outputs)
    start = (jnp.zeros((9 * C, C), jnp.float32), jnp.zeros((2 * C, C), jnp.float32))
    (sum_space, sum_temp), features = lax.scan(one_tile, start, (tile_view, cot_view, halo_flags, live_all))
    factor = 1.0 / jnp.sqrt(jnp.float32(N_DP * N_BAL * WORK_TILES))
    return (features, sum_space * factor, sum_temp * factor)
```

```python
import functools
import math

import jax
import jax.numpy as jnp
from jax import lax
from jax.experimental import pallas as pl
from jax.experimental.pallas import tpu as pltpu
from jax.sharding import PartitionSpec as P

FR, H, W = 6, 5, 9
TR, TC, TO = 2, 4, 4
WORK_TILES = 12
F32, BF16 = jnp.float32, jnp.bfloat16
MESH = pl.DeviceIdType.MESH


def up(value, step):
    return (value + step - 1) // step * step


def kernel(
    cfg,
    tiles_ref, cot_ref, flags_ref, plan_ref, wsp_ref, wtp_ref,
    feat_ref, grad_ref,
    tbuf, xf, cf, patches, cotp, wsp, wtp, act, dact, grad_t, cot_t, live, masks,
    own, s1, r1, s2, r2, own3, s3, r3,
    tile_sem, loc_sem, ag_send, ag_recv, fw_send, fw_recv,
    s1_send, s1_recv, s2_send, s2_recv, s3_send, s3_recv,
):
    nd, nb, owned, C = cfg["nd"], cfg["nb"], cfg["owned"], cfg["C"]
    S, rs, rt, nt, nl = cfg["S"], cfg["rs"], cfg["rt"], cfg["nt"], cfg["nl"]
    cw, cwp, parts = cfg["cw"], cfg["cwp"], cfg["parts"]
    nz = nd // 2
    cells, opix = FR * H * W, TO * TR * TC
    ts, cs = cells + 1, opix + 1
    FS = TR * TC * S
    half = C // 2

    d = lax.axis_index("dp")
    b = lax.axis_index("bal")
    core = lax.rem(d, 2)
    z = d // 2
    mate = d + 1 - 2 * core

    def bal_peer(k):
        return lax.rem(b + k, nb)

    def z_peer(k):
        return lax.rem(z + k, nz)

    tile_copies = []
    lo = 0
    for n, count in enumerate(parts):
        cp = pltpu.make_async_copy(
            tiles_ref.at[pl.ds(lo, count)], tbuf.at[pl.ds(lo, count)], tile_sem.at[n]
        )
        cp.start()
        tile_copies.append((cp, lo, count))
        lo += count
    my_sp = pl.ds(pl.multiple_of(b * rs, 16), rs)
    my_tp = pl.ds(pl.multiple_of(b * rt, 16), rt)
    local = [
        pltpu.make_async_copy(wsp_ref, wsp.at[my_sp], loc_sem.at[0]),
        pltpu.make_async_copy(wtp_ref, wtp.at[my_tp], loc_sem.at[1]),
    ]
    for cp in local:
        cp.start()

    barrier = pltpu.get_barrier_semaphore()
    pl.semaphore_signal(barrier, inc=1, device_id=(mate, b), device_id_type=MESH)
    for k in range(1, nb):
        pl.semaphore_signal(barrier, inc=1, device_id=(d, bal_peer(k)), device_id_type=MESH)
    for k in range(1, nz):
        pl.semaphore_signal(
            barrier, inc=1, device_id=(2 * z_peer(k) + core, b), device_id_type=MESH
        )
    pl.semaphore_wait(barrier, nb + nz - 1)

    lanes = pl.ds(pl.multiple_of(core * half, 128), half)
    gathers = []
    for k in range(1, nb):
        for n, (src, dst, rows) in enumerate(((wsp_ref, wsp, my_sp), (wtp_ref, wtp, my_tp))):
            cp = pltpu.make_async_remote_copy(
                src_ref=src.at[:, lanes],
                dst_ref=dst.at[rows, lanes],
                send_sem=ag_send.at[n, k - 1],
                recv_sem=ag_recv.at[n, k - 1],
                device_id=(d, bal_peer(k)),
                device_id_type=MESH,
            )
            cp.start()
            gathers.append(cp)

    masks[...] = jnp.zeros_like(masks)
    flags = flags_ref[...]
    for n in range(3):
        masks[n, 0:owned, :] = jnp.broadcast_to(
            (flags[:, n : n + 1] > 0).astype(F32), (owned, 128)
        )
    slot = lax.broadcasted_iota(jnp.int32, (S, 128), 0)
    found = jnp.zeros((S, 128), F32)
    for w in range(plan_ref.shape[1]):
        for q in range(plan_ref.shape[2]):
            found = jnp.maximum(found, jnp.where(slot == plan_ref[0, w, q], 1.0, 0.0))
    live[...] = found

    if S > owned:
        for h in range(2):
            cf[h, owned * cs : S * cs, :] = jnp.zeros(((S - owned) * cs, 128), F32)
            xf[h, owned * ts : S * ts, :] = jnp.zeros(((S - owned) * ts, 128), F32)

    def cot_in(s, carry):
        v = cot_ref[s].astype(F32)
        for h in range(2):
            cf[h, pl.ds(s * cs, opix), :] = v[:, h * 128 : (h + 1) * 128]
        return carry

    lax.fori_loop(0, owned, cot_in, 0)
    lv = live[...]

    def cot_rows(p, carry):
        for h in range(2):
            pair = [
                cf[h, pl.ds(2 * p + n, S, stride=cs), :] * lv for n in range(2)
            ]
            cotp[pl.ds(pl.multiple_of(p * 2 * S, 16), 2 * S), h * 128 : (h + 1) * 128] = (
                jnp.concatenate(pair, axis=0).astype(BF16)
            )
        return carry

    lax.fori_loop(0, opix // 2, cot_rows, 0)

    def tile_in(s, carry):
        v = tbuf[s].astype(F32)
        for h in range(2):
            xf[h, pl.ds(s * ts, cells), :] = v[:, h * 128 : (h + 1) * 128]
        return carry

    for cp, lo, count in tile_copies:
        cp.wait()
        lax.fori_loop(lo, lo + count, tile_in, 0)

    top, left, past = masks[0], masks[1], masks[2]

    def patch_rows(f, carry):
        hist = jnp.where(f >= 2, jnp.ones_like(past), past)
        hist_top, hist_left = hist * top, hist * left
        hist_both = hist_top * left
        for i in range(TR):
            for jp in range(TC // 2):
                row = pl.ds(pl.multiple_of(f * FS + (i * TC + 2 * jp) * S, 16), 2 * S)
                for ky in range(3):
                    for kx in range(3):
                        on_top = 2 * i + ky == 0
                        on_left = jp == 0 and kx == 0
                        first = (
                            hist_both if on_top and on_left
                            else hist_top if on_top
                            else hist_left if on_left
                            else hist
                        )
                        second = hist_top if on_top else hist
                        cell = f * (H * W) + (2 * i + ky) * W + 4 * jp + kx
                        tap = 3 * ky + kx
                        for h in range(2):
                            v0 = xf[h, pl.ds(cell, S, stride=ts), :] * first
                            v1 = xf[h, pl.ds(cell + 2, S, stride=ts), :] * second
                            patches[row, tap * C + h * 128 : tap * C + (h + 1) * 128] = (
                                jnp.concatenate([v0, v1], axis=0).astype(BF16)
                            )
        return carry

    lax.fori_loop(0, FR, patch_rows, 0)

    def split_rows(v):
        cores = [
            jnp.concatenate(
                [v[(2 * n + q) * cw : (2 * n + q + 1) * cw] for n in range(nz)], axis=0
            )
            for q in range(2)
        ]
        return cores

    def store_split(ref, v, lo, width):
        cores = split_rows(v)
        for q in range(2):
            at = core if q == 1 else 0
            at = (1 - core) if q == 1 else core
            ref[pl.ds(pl.multiple_of(at * half, 128), half), lo : lo + width] = cores[
                q
            ].astype(BF16)

    for n in range(2):
        rows = n * 2 * FS
        store_split(cot_t, cotp[rows : rows + 2 * FS, :].astype(F32).T, rows, 2 * FS)

    for cp in local:
        cp.wait()
    forwards = []
    for k in range(1, nb):
        origin = lax.rem(b + nb - k, nb)
        for n, (dst, size) in enumerate(((wsp, rs), (wtp, rt))):
            gathers[2 * (k - 1) + n].wait_recv()
            rows = pl.ds(pl.multiple_of(origin * size, 16), size)
            cp = pltpu.make_async_remote_copy(
                src_ref=dst.at[rows, lanes],
                dst_ref=dst.at[rows, lanes],
                send_sem=fw_send.at[n, k - 1],
                recv_sem=fw_recv.at[n, k - 1],
                device_id=(mate, b),
                device_id_type=MESH,
            )
            cp.start()
            forwards.append(cp)
    for cp in forwards:
        cp.wait_recv()

    def chunk(n):
        rows = n * 2 * FS
        pre = jnp.dot(patches[rows : rows + 2 * FS, :], wsp[...], preferred_element_type=F32)
        sig = 1.0 / (1.0 + jnp.exp(-pre))
        act[rows : rows + 2 * FS, :] = (pre * sig).astype(BF16)
        ga = None
        nt_dims = (((1,), (1,)), ((), ()))
        if n > 0:
            lo = (n - 1) * 2 * FS
            ga = lax.dot_general(
                cotp[lo : lo + 2 * FS, :], wtp[0:C, :], nt_dims, preferred_element_type=F32
            )
        if n < 2:
            g = lax.dot_general(
                cotp[rows : rows + 2 * FS, :], wtp[C : 2 * C, :], nt_dims,
                preferred_element_type=F32,
            )
            ga = g if ga is None else ga + g
        gp = ga * (sig * (1.0 + pre * (1.0 - sig)))
        store_split(grad_t, gp.T, rows, 2 * FS)

    for n in range(3):
        chunk(n)

    sp_lanes = nt * 128

    def section(k):
        to = bal_peer(k)
        sp_at = pl.multiple_of((to * rs) // 128 * 128, 128)
        g = jnp.dot(grad_t[...], patches[:, pl.ds(sp_at, sp_lanes)], preferred_element_type=F32)
        own[k - 1, :, 0:sp_lanes] = g[0:half]
        s1[k - 1, :, 0:sp_lanes] = g[half:].astype(BF16)
        tp_at = (to * rt) // 128 * 128
        tap = tp_at // C
        at = pl.multiple_of(tp_at - tap * C, 128)
        rows = pl.ds(pl.multiple_of((1 - tap) * 2 * FS, 16), TO * FS)
        g = jnp.dot(cot_t[...], act[rows, pl.ds(at, 128)], preferred_element_type=F32)
        own[k - 1, :, sp_lanes:] = g[0:half]
        s1[k - 1, :, sp_lanes:] = g[half:].astype(BF16)
        cp = pltpu.make_async_remote_copy(
            src_ref=s1.at[k - 1], dst_ref=r1.at[k - 1],
            send_sem=s1_send.at[k - 1], recv_sem=s1_recv.at[k - 1],
            device_id=(mate, b), device_id_type=MESH,
        )
        cp.start()
        return cp

    first = {}
    second = {}

    def pass_on(k):
        first[k].wait_recv()
        total = own[k - 1] + r1[k - 1].astype(F32)
        if k == nb:
            own[k - 1] = total
            return
        s2[k - 1] = total.astype(BF16)
        cp = pltpu.make_async_remote_copy(
            src_ref=s2.at[k - 1], dst_ref=r2.at[k - 1],
            send_sem=s2_send.at[k - 1], recv_sem=s2_recv.at[k - 1],
            device_id=(d, bal_peer(k)), device_id_type=MESH,
        )
        cp.start()
        second[k] = cp

    for k in range(1, nb + 1):
        first[k] = section(k)
        if k > 1:
            pass_on(k - 1)
    pass_on(nb)

    def features(t0):
        rows = t0 * FS
        feat = jnp.dot(
            act[rows + 2 * FS : rows + 4 * FS, :], wtp[0:C, :], preferred_element_type=F32
        ) + jnp.dot(act[rows : rows + 2 * FS, :], wtp[C : 2 * C, :], preferred_element_type=F32)
        for p in range(2 * TR * TC):
            for h in range(2):
                v = feat[p * S : (p + 1) * S, h * 128 : (h + 1) * 128]
                cf[h, pl.ds(t0 * TR * TC + p, S, stride=cs), :] = v * lv

    features(0)
    features(2)

    def feat_out(s, carry):
        feat_ref[s] = jnp.concatenate(
            [cf[h, pl.ds(s * cs, opix), :] for h in range(2)], axis=1
        ).astype(BF16)
        return carry

    lax.fori_loop(0, owned, feat_out, 0)

    total = own[nb - 1]
    for k in range(1, nb):
        second[k].wait_recv()
        total = total + r2[k - 1].astype(F32)
    for n in range(nz):
        part = total[n * cw : (n + 1) * cw]
        own3[n] = part
        if cwp > cw:
            part = jnp.concatenate([part, jnp.zeros((cwp - cw, nl), F32)], axis=0)
        s3[n] = part.astype(BF16)
    third = []
    for k in range(1, nz):
        to = z_peer(k)
        cp = pltpu.make_async_remote_copy(
            src_ref=s3.at[to], dst_ref=r3.at[k - 1],
            send_sem=s3_send.at[k - 1], recv_sem=s3_recv.at[k - 1],
            device_id=(2 * to + core, b), device_id_type=MESH,
        )
        cp.start()
        third.append(cp)
    total = own3[z]
    for k in range(1, nz):
        third[k - 1].wait_recv()
        total = total + r3[k - 1].astype(F32)[0:cw]
    grad_ref[...] = total * cfg["factor"]

    for cp in gathers + forwards + list(first.values()) + list(second.values()) + third:
        cp.wait_send()


def per_device(tiles, cotangent, halo_flags, send_plan, spatial_weight, temporal_weight):
    nd, nb = lax.axis_size("dp"), lax.axis_size("bal")
    owned, cells, C = tiles.shape
    opix = cotangent.shape[1]
    rs, rt = spatial_weight.shape[0], temporal_weight.shape[0]
    S = up(owned, 8)
    nt = max(-(-(rs * (n + 1)) // 128) - rs * n // 128 for n in range(nb))
    sp_lanes = nt * 128
    nl = sp_lanes + 128
    cw = C // nd
    cwp = up(cw, 16)
    nz = nd // 2
    half = C // 2
    n_parts = 4
    parts = [owned // n_parts + (n < owned % n_parts) for n in range(n_parts)]
    cfg = dict(
        nd=nd, nb=nb, owned=owned, C=C, S=S, rs=rs, rt=rt, nt=nt, nl=nl, cw=cw, cwp=cwp,
        parts=parts, factor=1.0 / math.sqrt(nd * nb * WORK_TILES),
    )
    M = FR * TR * TC * S
    K = TO * TR * TC * S
    vm = pltpu.VMEM
    dma = pltpu.SemaphoreType.DMA
    any_spec = pl.BlockSpec(memory_space=pl.ANY)
    vspec = pl.BlockSpec(memory_space=pltpu.VMEM)
    scratch = [
        vm((owned, cells, C), BF16),
        vm((2, S * (cells + 1), 128), F32),
        vm((2, S * (opix + 1), 128), F32),
        vm((M, 9 * C), BF16),
        vm((K, C), BF16),
        vm((9 * C, C), BF16),
        vm((2 * C, C), BF16),
        vm((M, C), BF16),
        vm((8, 128), F32),
        vm((C, M), BF16),
        vm((C, K), BF16),
        vm((S, 128), F32),
        vm((3, S, 128), F32),
        vm((nb, half, nl), F32),
        vm((nb, half, nl), BF16),
        vm((nb, half, nl), BF16),
        vm((nb - 1, half, nl), BF16),
        vm((nb - 1, half, nl), BF16),
        vm((nz, cw, nl), F32),
        vm((nz, cwp, nl), BF16),
        vm((nz - 1, cwp, nl), BF16),
        dma((n_parts,)),
        dma((2,)),
        dma((2, nb - 1)), dma((2, nb - 1)), dma((2, nb - 1)), dma((2, nb - 1)),
        dma((nb,)), dma((nb,)),
        dma((nb - 1,)), dma((nb - 1,)),
        dma((nz - 1,)), dma((nz - 1,)),
    ]
    features, grads = pl.pallas_call(
        functools.partial(kernel, cfg),
        out_shape=(
            jax.ShapeDtypeStruct((owned, opix, C), BF16),
            jax.ShapeDtypeStruct((cw, nl), F32),
        ),
        in_specs=[
            any_spec, vspec, vspec, pl.BlockSpec(memory_space=pltpu.SMEM), any_spec, any_spec,
        ],
        out_specs=(vspec, vspec),
        scratch_shapes=scratch,
        compiler_params=pltpu.CompilerParams(
            collective_id=0, has_side_effects=True, vmem_limit_bytes=50 * 1024 * 1024
        ),
    )(tiles, cotangent, halo_flags, send_plan, spatial_weight, temporal_weight)
    b = lax.axis_index("bal")
    sp = lax.dynamic_slice(grads, (0, lax.rem(b * rs, 128)), (cw, rs)).T
    tp = lax.dynamic_slice(grads, (0, sp_lanes + lax.rem(b * rt, 128)), (cw, rt)).T
    return (features, sp, tp)


def solution(mesh):
    in_specs = (
        P(("dp", "bal"), None, None),
        P(("dp", "bal"), None, None),
        P(("dp", "bal"), None),
        P(("dp", "bal"), None, None),
        P("bal", None),
        P("bal", None),
    )
    out_specs = (P(("dp", "bal"), None, None), P("bal", "dp"), P("bal", "dp"))
    return jax.shard_map(
        per_device, mesh=mesh, in_specs=in_specs, out_specs=out_specs, check_vma=False
    )
```

```python
import functools
import math

import jax
import jax.numpy as jnp
from jax import lax
from jax.experimental import pallas as pl
from jax.experimental.pallas import tpu as pltpu
from jax.sharding import PartitionSpec as P

FR, H, W = 6, 5, 9
TR, TC, TO = 2, 4, 4
WORK_TILES = 12
F32, BF16 = jnp.float32, jnp.bfloat16
MESH = pl.DeviceIdType.MESH


def up(value, step):
    return (value + step - 1) // step * step


def kernel(
    cfg,
    tiles_ref, cot_ref, flags_ref, plan_ref, wsp_ref, wtp_ref,
    feat_ref, grad_ref,
    cbuf, fbuf, pbuf, ftmp, tbuf, xf, cf, patches, cotp, wsp, wtp, act, dact, grad_t, cot_t, live, masks,
    own, s1, r1, s2, r2, own3, s3, r3,
    tile_sem, loc_sem, ag_send, ag_recv, zr_send, zr_recv, fw_send, fw_recv,
    s1_send, s1_recv, s2_send, s2_recv, s3_send, s3_recv,
):
    nd, nb, owned, C = cfg["nd"], cfg["nb"], cfg["owned"], cfg["C"]
    S, rs, rt, nt, nl = cfg["S"], cfg["rs"], cfg["rt"], cfg["nt"], cfg["nl"]
    cw, cwp, parts = cfg["cw"], cfg["cwp"], cfg["parts"]
    nz = nd // 2
    cells, opix = FR * H * W, TO * TR * TC
    ts, cs = cells + 1, opix + 1
    FS = TR * TC * S
    half = C // 2

    d = lax.axis_index("dp")
    b = lax.axis_index("bal")
    core = lax.rem(d, 2)
    z = d // 2
    mate = d + 1 - 2 * core

    def bal_peer(k):
        return lax.rem(b + k, nb)

    def z_peer(k):
        return lax.rem(z + k, nz)

    def local_copy(src, dst, sem):
        cp = pltpu.make_async_copy(src, dst, sem)
        cp.start()
        return cp

    barrier = pltpu.get_barrier_semaphore()
    pl.semaphore_signal(barrier, inc=1, device_id=(mate, b), device_id_type=MESH)
    for k in range(1, nb):
        pl.semaphore_signal(barrier, inc=1, device_id=(d, bal_peer(k)), device_id_type=MESH)
    for k in range(1, nz):
        pl.semaphore_signal(
            barrier, inc=1, device_id=(2 * z_peer(k) + core, b), device_id_type=MESH
        )

    small_copies = [
        local_copy(flags_ref, fbuf, loc_sem.at[2]),
        local_copy(plan_ref, pbuf, loc_sem.at[3]),
        local_copy(cot_ref, cbuf, loc_sem.at[4]),
    ]
    tile_copies = []
    lo = 0
    for n, count in enumerate(parts):
        part = pl.ds(lo, count)
        cp = local_copy(tiles_ref.at[part], tbuf.at[part], tile_sem.at[n])
        tile_copies.append((cp, lo, count))
        lo += count
    my_sp = pl.ds(pl.multiple_of(b * rs, 16), rs)
    my_tp = pl.ds(pl.multiple_of(b * rt, 16), rt)
    local = [
        local_copy(wsp_ref, wsp.at[my_sp], loc_sem.at[0]),
        local_copy(wtp_ref, wtp.at[my_tp], loc_sem.at[1]),
    ]

    if S > owned:
        for h in range(2):
            cf[h, owned * cs : S * cs, :] = jnp.zeros(((S - owned) * cs, 128), F32)
            xf[h, owned * ts : S * ts, :] = jnp.zeros(((S - owned) * ts, 128), F32)

    pl.semaphore_wait(barrier, nb + nz - 1)

    lanes = pl.ds(pl.multiple_of(core * half, 128), half)
    zpar = lax.rem(z, 2)
    zmate = 2 * (z + 1 - 2 * zpar) + core
    weights = []
    for src, dst, size in ((wsp_ref, wsp, rs), (wtp_ref, wtp, rt)):
        units = size // 16
        fetch = units if nz % 2 else max((units + 1) // 2, round(0.6 * units))
        weights.append((src, dst, size, fetch * 16, (units - fetch) * 16))

    def rows_at(start, count):
        return pl.ds(pl.multiple_of(start, 16), count)

    gathers, relays, forwards = {}, {}, {}
    for k in range(1, nb):
        for n, (src, dst, size, fetch, rest) in enumerate(weights):
            cp = pltpu.make_async_remote_copy(
                src_ref=src.at[rows_at(zpar * rest, fetch), lanes],
                dst_ref=dst.at[rows_at(b * size + zpar * rest, fetch), lanes],
                send_sem=ag_send.at[n, k - 1],
                recv_sem=ag_recv.at[n, k - 1],
                device_id=(d, bal_peer(k)),
                device_id_type=MESH,
            )
            cp.start()
            gathers[n, k] = cp

    def push(ref, rows, to, send, recv):
        cp = pltpu.make_async_remote_copy(
            src_ref=ref.at[rows, lanes], dst_ref=ref.at[rows, lanes],
            send_sem=send, recv_sem=recv, device_id=(to, b), device_id_type=MESH,
        )
        cp.start()
        return cp

    def relay(k):
        origin = lax.rem(b + nb - k, nb)
        for n, (src, dst, size, fetch, rest) in enumerate(weights):
            gathers[n, k].wait_recv()
            if rest:
                relays[n, k] = push(
                    dst, rows_at(origin * size + zpar * fetch, rest), zmate,
                    zr_send.at[n, k - 1], zr_recv.at[n, k - 1],
                )
            forwards[0, n, k] = push(
                dst, rows_at(origin * size + zpar * rest, fetch), mate,
                fw_send.at[0, n, k - 1], fw_recv.at[0, n, k - 1],
            )

    def relay_rest(k):
        origin = lax.rem(b + nb - k, nb)
        for n, (src, dst, size, fetch, rest) in enumerate(weights):
            if rest:
                relays[n, k].wait_recv()
                forwards[1, n, k] = push(
                    dst, rows_at(origin * size + (1 - zpar) * fetch, rest), mate,
                    fw_send.at[1, n, k - 1], fw_recv.at[1, n, k - 1],
                )

    for cp in small_copies:
        cp.wait()
    slot = lax.broadcasted_iota(jnp.int32, (S, 128), 0)
    lane = lax.broadcasted_iota(jnp.int32, (S, 128), 1)
    ftmp[...] = jnp.zeros_like(ftmp)
    ftmp[0:3, 0:owned] = (fbuf[...] > 0).astype(F32)
    for n in range(3):
        row = jnp.broadcast_to(ftmp[n : n + 1, :], (S, 128))
        column = jnp.sum(jnp.where(slot == lane, row, 0.0), axis=1, keepdims=True)
        masks[n] = jnp.broadcast_to(column, (S, 128))
    found = jnp.zeros((S, 128), F32)
    for w in range(pbuf.shape[1]):
        for q in range(pbuf.shape[2]):
            found = jnp.maximum(found, jnp.where(slot == pbuf[0, w, q], 1.0, 0.0))
    live[...] = found

    def cot_in(s, carry):
        v = cbuf[s].astype(F32)
        for h in range(2):
            cf[h, pl.ds(s * cs, opix), :] = v[:, h * 128 : (h + 1) * 128]
        return carry

    lax.fori_loop(0, owned, cot_in, 0)
    lv = live[...]

    def cot_rows(p, carry):
        for h in range(2):
            pair = [
                cf[h, pl.ds(2 * p + n, S, stride=cs), :] * lv for n in range(2)
            ]
            cotp[pl.ds(pl.multiple_of(p * 2 * S, 16), 2 * S), h * 128 : (h + 1) * 128] = (
                jnp.concatenate(pair, axis=0).astype(BF16)
            )
        return carry

    lax.fori_loop(0, opix // 2, cot_rows, 0)

    def split_rows(v):
        cores = [
            jnp.concatenate(
                [v[(2 * n + q) * cw : (2 * n + q + 1) * cw] for n in range(nz)], axis=0
            )
            for q in range(2)
        ]
        return cores

    def store_split(ref, v, lo, width):
        cores = split_rows(v)
        for q in range(2):
            at = core if q == 1 else 0
            at = (1 - core) if q == 1 else core
            ref[pl.ds(pl.multiple_of(at * half, 128), half), lo : lo + width] = cores[
                q
            ].astype(BF16)

    for n in range(2):
        rows = n * 2 * FS
        store_split(cot_t, cotp[rows : rows + 2 * FS, :].astype(F32).T, rows, 2 * FS)

    def tile_in(s, carry):
        v = tbuf[s].astype(F32)
        for h in range(2):
            xf[h, pl.ds(s * ts, cells), :] = v[:, h * 128 : (h + 1) * 128]
        return carry

    for cp, lo, count in tile_copies:
        cp.wait()
        lax.fori_loop(lo, lo + count, tile_in, 0)

    top, left, past = masks[0], masks[1], masks[2]

    def patch_rows(f, carry):
        hist = jnp.where(f >= 2, jnp.ones_like(past), past)
        hist_top, hist_left = hist * top, hist * left
        hist_both = hist_top * left
        for i in range(TR):
            for jp in range(TC // 2):
                row = pl.ds(pl.multiple_of(f * FS + (i * TC + 2 * jp) * S, 16), 2 * S)
                for ky in range(3):
                    for kx in range(3):
                        on_top = 2 * i + ky == 0
                        on_left = jp == 0 and kx == 0
                        first = (
                            hist_both if on_top and on_left
                            else hist_top if on_top
                            else hist_left if on_left
                            else hist
                        )
                        second = hist_top if on_top else hist
                        cell = f * (H * W) + (2 * i + ky) * W + 4 * jp + kx
                        tap = 3 * ky + kx
                        for h in range(2):
                            v0 = xf[h, pl.ds(cell, S, stride=ts), :] * first
                            v1 = xf[h, pl.ds(cell + 2, S, stride=ts), :] * second
                            patches[row, tap * C + h * 128 : tap * C + (h + 1) * 128] = (
                                jnp.concatenate([v0, v1], axis=0).astype(BF16)
                            )
        return carry

    steps = max(nb - 1, 1)
    cuts = [FR * n // steps for n in range(steps + 1)]
    for n in range(steps):
        if cuts[n + 1] > cuts[n]:
            lax.fori_loop(cuts[n], cuts[n + 1], patch_rows, 0)
        if n + 1 < nb:
            relay(n + 1)
    for k in range(1, nb):
        relay_rest(k)
    for cp in local:
        cp.wait()
    for cp in forwards.values():
        cp.wait_recv()

    def chunk(n):
        rows = n * 2 * FS
        pre = jnp.dot(patches[rows : rows + 2 * FS, :], wsp[...], preferred_element_type=F32)
        sig = 1.0 / (1.0 + jnp.exp(-pre))
        act[rows : rows + 2 * FS, :] = (pre * sig).astype(BF16)
        ga = None
        nt_dims = (((1,), (1,)), ((), ()))
        if n > 0:
            lo = (n - 1) * 2 * FS
            ga = lax.dot_general(
                cotp[lo : lo + 2 * FS, :], wtp[0:C, :], nt_dims, preferred_element_type=F32
            )
        if n < 2:
            g = lax.dot_general(
                cotp[rows : rows + 2 * FS, :], wtp[C : 2 * C, :], nt_dims,
                preferred_element_type=F32,
            )
            ga = g if ga is None else ga + g
        gp = ga * (sig * (1.0 + pre * (1.0 - sig)))
        store_split(grad_t, gp.T, rows, 2 * FS)

    for n in range(3):
        chunk(n)

    sp_lanes = nt * 128
    cut = (nt + 2) // 2
    spans = [(0, cut), (cut, nt)]
    bounds = [pl.ds(0, cut * 128), pl.ds(cut * 128, nl - cut * 128)]

    def section(h, k):
        to = bal_peer(k)
        lo, hi = spans[h]
        if hi > lo:
            sp_at = pl.multiple_of((to * rs) // 128 * 128 + lo * 128, 128)
            g = jnp.dot(
                grad_t[...], patches[:, pl.ds(sp_at, (hi - lo) * 128)],
                preferred_element_type=F32,
            )
            own[k - 1, :, lo * 128 : hi * 128] = g[0:half]
            s1[k - 1, :, lo * 128 : hi * 128] = g[half:].astype(BF16)
        if h == 1:
            tp_at = (to * rt) // 128 * 128
            tap = tp_at // C
            at = pl.multiple_of(tp_at - tap * C, 128)
            rows = pl.ds(pl.multiple_of((1 - tap) * 2 * FS, 16), TO * FS)
            g = jnp.dot(cot_t[...], act[rows, pl.ds(at, 128)], preferred_element_type=F32)
            own[k - 1, :, sp_lanes:] = g[0:half]
            s1[k - 1, :, sp_lanes:] = g[half:].astype(BF16)
        cp = pltpu.make_async_remote_copy(
            src_ref=s1.at[k - 1, :, bounds[h]], dst_ref=r1.at[k - 1, :, bounds[h]],
            send_sem=s1_send.at[h, k - 1], recv_sem=s1_recv.at[h, k - 1],
            device_id=(mate, b), device_id_type=MESH,
        )
        cp.start()
        first[h, k] = cp

    first, second, third = {}, {}, {}

    def pass_on(h, k):
        first[h, k].wait_recv()
        at = bounds[h]
        total = own[k - 1, :, at] + r1[k - 1, :, at].astype(F32)
        if k == nb:
            own[k - 1, :, at] = total
            return
        s2[k - 1, :, at] = total.astype(BF16)
        cp = pltpu.make_async_remote_copy(
            src_ref=s2.at[k - 1, :, at], dst_ref=r2.at[k - 1, :, at],
            send_sem=s2_send.at[h, k - 1], recv_sem=s2_recv.at[h, k - 1],
            device_id=(d, bal_peer(k)), device_id_type=MESH,
        )
        cp.start()
        second[h, k] = cp

    order = [(h, k) for h in range(2) for k in range(1, nb + 1)]
    for n, unit in enumerate(order):
        section(*unit)
        if n > 0:
            pass_on(*order[n - 1])
    pass_on(*order[-1])

    def features(t0):
        rows = t0 * FS
        feat = jnp.dot(
            act[rows + 2 * FS : rows + 4 * FS, :], wtp[0:C, :], preferred_element_type=F32
        ) + jnp.dot(act[rows : rows + 2 * FS, :], wtp[C : 2 * C, :], preferred_element_type=F32)
        for p in range(2 * TR * TC):
            for h in range(2):
                v = feat[p * S : (p + 1) * S, h * 128 : (h + 1) * 128]
                cf[h, pl.ds(t0 * TR * TC + p, S, stride=cs), :] = v * lv

    def group_sum(h):
        at = bounds[h]
        total = own[nb - 1, :, at]
        for k in range(1, nb):
            second[h, k].wait_recv()
            total = total + r2[k - 1, :, at].astype(F32)
        for n in range(nz):
            part = total[n * cw : (n + 1) * cw]
            own3[n, :, at] = part
            if cwp > cw:
                part = jnp.concatenate(
                    [part, jnp.zeros((cwp - cw, part.shape[1]), F32)], axis=0
                )
            s3[n, :, at] = part.astype(BF16)
        for k in range(1, nz):
            to = z_peer(k)
            cp = pltpu.make_async_remote_copy(
                src_ref=s3.at[to, :, at], dst_ref=r3.at[k - 1, :, at],
                send_sem=s3_send.at[h, k - 1], recv_sem=s3_recv.at[h, k - 1],
                device_id=(2 * to + core, b), device_id_type=MESH,
            )
            cp.start()
            third[h, k] = cp

    features(0)
    features(2)
    group_sum(0)

    def feat_out(s, carry):
        cbuf[s] = jnp.concatenate(
            [cf[h, pl.ds(s * cs, opix), :] for h in range(2)], axis=1
        ).astype(BF16)
        return carry

    lax.fori_loop(0, owned, feat_out, 0)
    feat_copy = local_copy(cbuf, feat_ref, loc_sem.at[5])
    group_sum(1)
    for h in range(2):
        at = bounds[h]
        total = own3[z, :, at]
        for k in range(1, nz):
            third[h, k].wait_recv()
            total = total + r3[k - 1, :, at].astype(F32)[0:cw]
        grad_ref[:, at] = total * cfg["factor"]

    feat_copy.wait()
    for group in (gathers, relays, forwards, first, second, third):
        for cp in group.values():
            cp.wait_send()


def per_device(tiles, cotangent, halo_flags, send_plan, spatial_weight, temporal_weight):
    nd, nb = lax.axis_size("dp"), lax.axis_size("bal")
    owned, cells, C = tiles.shape
    opix = cotangent.shape[1]
    rs, rt = spatial_weight.shape[0], temporal_weight.shape[0]
    S = up(owned, 8)
    nt = max(-(-(rs * (n + 1)) // 128) - rs * n // 128 for n in range(nb))
    sp_lanes = nt * 128
    nl = sp_lanes + 128
    cw = C // nd
    cwp = up(cw, 16)
    nz = nd // 2
    half = C // 2
    n_parts = 4
    parts = [owned // n_parts + (n < owned % n_parts) for n in range(n_parts)]
    cfg = dict(
        nd=nd, nb=nb, owned=owned, C=C, S=S, rs=rs, rt=rt, nt=nt, nl=nl, cw=cw, cwp=cwp,
        parts=parts, factor=1.0 / math.sqrt(nd * nb * WORK_TILES),
    )
    M = FR * TR * TC * S
    K = TO * TR * TC * S
    vm = pltpu.VMEM
    dma = pltpu.SemaphoreType.DMA
    hbm = pl.BlockSpec(memory_space=pltpu.HBM)
    vspec = pl.BlockSpec(memory_space=pltpu.VMEM)
    scratch = [
        vm((owned, opix, C), BF16),
        vm((3, owned), jnp.int32),
        pltpu.SMEM(send_plan.shape, jnp.int32),
        vm((8, 128), F32),
        vm((owned, cells, C), BF16),
        vm((2, S * (cells + 1), 128), F32),
        vm((2, S * (opix + 1), 128), F32),
        vm((M, 9 * C), BF16),
        vm((K, C), BF16),
        vm((9 * C, C), BF16),
        vm((2 * C, C), BF16),
        vm((M, C), BF16),
        vm((8, 128), F32),
        vm((C, M), BF16),
        vm((C, K), BF16),
        vm((S, 128), F32),
        vm((3, S, 128), F32),
        vm((nb, half, nl), F32),
        vm((nb, half, nl), BF16),
        vm((nb, half, nl), BF16),
        vm((nb - 1, half, nl), BF16),
        vm((nb - 1, half, nl), BF16),
        vm((nz, cw, nl), F32),
        vm((nz, cwp, nl), BF16),
        vm((nz - 1, cwp, nl), BF16),
        dma((n_parts,)),
        dma((6,)),
        dma((2, nb - 1)), dma((2, nb - 1)), dma((2, nb - 1)), dma((2, nb - 1)),
        dma((2, 2, nb - 1)), dma((2, 2, nb - 1)),
        dma((2, nb)), dma((2, nb)),
        dma((2, nb - 1)), dma((2, nb - 1)),
        dma((2, nz - 1)), dma((2, nz - 1)),
    ]
    features, grads = pl.pallas_call(
        functools.partial(kernel, cfg),
        out_shape=(
            jax.ShapeDtypeStruct((owned, opix, C), BF16),
            jax.ShapeDtypeStruct((cw, nl), F32),
        ),
        in_specs=[hbm] * 6,
        out_specs=(hbm, vspec),
        scratch_shapes=scratch,
        compiler_params=pltpu.CompilerParams(
            collective_id=0, has_side_effects=True, vmem_limit_bytes=64 * 1024 * 1024 - 65536
        ),
    )(tiles, cotangent, halo_flags.T, send_plan, spatial_weight, temporal_weight)
    b = lax.axis_index("bal")
    sp = lax.dynamic_slice(grads, (0, lax.rem(b * rs, 128)), (cw, rs)).T
    tp = lax.dynamic_slice(grads, (0, sp_lanes + lax.rem(b * rt, 128)), (cw, rt)).T
    return (features, sp, tp)


def solution(mesh):
    in_specs = (
        P(("dp", "bal"), None, None),
        P(("dp", "bal"), None, None),
        P(("dp", "bal"), None),
        P(("dp", "bal"), None, None),
        P("bal", None),
        P("bal", None),
    )
    out_specs = (P(("dp", "bal"), None, None), P("bal", "dp"), P("bal", "dp"))
    return jax.shard_map(
        per_device, mesh=mesh, in_specs=in_specs, out_specs=out_specs, check_vma=False
    )
```

```python
import functools
import math

import jax
import jax.numpy as jnp
from jax import lax
from jax.experimental import pallas as pl
from jax.experimental.pallas import tpu as pltpu
from jax.sharding import PartitionSpec as P

FR, H, W = 6, 5, 9
TR, TC, TO = 2, 4, 4
WORK_TILES = 12
F32, BF16 = jnp.float32, jnp.bfloat16
MESH = pl.DeviceIdType.MESH


def up(value, step):
    return (value + step - 1) // step * step


def kernel(
    cfg,
    tiles_ref, cot_ref, flags_ref, plan_ref, wsp_ref, wtp_ref,
    feat_ref, grad_ref,
    cbuf, fbuf, pbuf, ftmp, tbuf, xf, cf, patches, cotp, wsp, wtp, act, dact, grad_t, cot_t, live, masks,
    own, s1, r1, s2, r2, own3, s3, r3,
    tile_sem, loc_sem, ag_send, ag_recv, zr_send, zr_recv, fw_send, fw_recv,
    s1_send, s1_recv, s2_send, s2_recv, s3_send, s3_recv,
):
    nd, nb, owned, C = cfg["nd"], cfg["nb"], cfg["owned"], cfg["C"]
    S, rs, rt, nt, nl = cfg["S"], cfg["rs"], cfg["rt"], cfg["nt"], cfg["nl"]
    cw, cwp, parts = cfg["cw"], cfg["cwp"], cfg["parts"]
    nz = nd // 2
    cells, opix = FR * H * W, TO * TR * TC
    ts, cs = cells + 1, opix + 1
    FS = TR * TC * S
    half = C // 2

    d = lax.axis_index("dp")
    b = lax.axis_index("bal")
    core = lax.rem(d, 2)
    z = d // 2
    mate = d + 1 - 2 * core

    def bal_peer(k):
        return lax.rem(b + k, nb)

    def z_peer(k):
        return lax.rem(z + k, nz)

    def local_copy(src, dst, sem):
        cp = pltpu.make_async_copy(src, dst, sem)
        cp.start()
        return cp

    barrier = pltpu.get_barrier_semaphore()
    pl.semaphore_signal(barrier, inc=1, device_id=(mate, b), device_id_type=MESH)
    for k in range(1, nb):
        pl.semaphore_signal(barrier, inc=1, device_id=(d, bal_peer(k)), device_id_type=MESH)
    for k in range(1, nz):
        pl.semaphore_signal(
            barrier, inc=1, device_id=(2 * z_peer(k) + core, b), device_id_type=MESH
        )

    small_copies = [
        local_copy(flags_ref, fbuf, loc_sem.at[2]),
        local_copy(plan_ref, pbuf, loc_sem.at[3]),
        local_copy(cot_ref, cbuf, loc_sem.at[4]),
    ]
    tile_copies = []
    lo = 0
    for n, count in enumerate(parts):
        part = pl.ds(lo, count)
        cp = local_copy(tiles_ref.at[part], tbuf.at[part], tile_sem.at[n])
        tile_copies.append((cp, lo, count))
        lo += count
    my_sp = pl.ds(pl.multiple_of(b * rs, 16), rs)
    my_tp = pl.ds(pl.multiple_of(b * rt, 16), rt)
    local = [
        local_copy(wsp_ref, wsp.at[my_sp], loc_sem.at[0]),
        local_copy(wtp_ref, wtp.at[my_tp], loc_sem.at[1]),
    ]

    if S > owned:
        for h in range(2):
            cf[h, owned * cs : S * cs, :] = jnp.zeros(((S - owned) * cs, 128), F32)
            xf[h, owned * ts : S * ts, :] = jnp.zeros(((S - owned) * ts, 128), F32)

    pl.semaphore_wait(barrier, nb + nz - 1)

    lanes = pl.ds(pl.multiple_of(core * half, 128), half)
    zpar = lax.rem(z, 2)
    zmate = 2 * (z + 1 - 2 * zpar) + core
    weights = []
    for src, dst, size in ((wsp_ref, wsp, rs), (wtp_ref, wtp, rt)):
        units = size // 16
        fetch = units if nz % 2 else max((units + 1) // 2, round(0.6 * units))
        weights.append((src, dst, size, fetch * 16, (units - fetch) * 16))

    def rows_at(start, count):
        return pl.ds(pl.multiple_of(start, 16), count)

    gathers, relays, forwards = {}, {}, {}
    for k in range(1, nb):
        for n, (src, dst, size, fetch, rest) in enumerate(weights):
            cp = pltpu.make_async_remote_copy(
                src_ref=src.at[rows_at(zpar * rest, fetch), lanes],
                dst_ref=dst.at[rows_at(b * size + zpar * rest, fetch), lanes],
                send_sem=ag_send.at[n, k - 1],
                recv_sem=ag_recv.at[n, k - 1],
                device_id=(d, bal_peer(k)),
                device_id_type=MESH,
            )
            cp.start()
            gathers[n, k] = cp

    def push(ref, rows, to, send, recv):
        cp = pltpu.make_async_remote_copy(
            src_ref=ref.at[rows, lanes], dst_ref=ref.at[rows, lanes],
            send_sem=send, recv_sem=recv, device_id=(to, b), device_id_type=MESH,
        )
        cp.start()
        return cp

    def relay(k):
        origin = lax.rem(b + nb - k, nb)
        for n, (src, dst, size, fetch, rest) in enumerate(weights):
            gathers[n, k].wait_recv()
            if rest:
                relays[n, k] = push(
                    dst, rows_at(origin * size + zpar * fetch, rest), zmate,
                    zr_send.at[n, k - 1], zr_recv.at[n, k - 1],
                )
            forwards[0, n, k] = push(
                dst, rows_at(origin * size + zpar * rest, fetch), mate,
                fw_send.at[0, n, k - 1], fw_recv.at[0, n, k - 1],
            )

    def relay_rest(k):
        origin = lax.rem(b + nb - k, nb)
        for n, (src, dst, size, fetch, rest) in enumerate(weights):
            if rest:
                relays[n, k].wait_recv()
                forwards[1, n, k] = push(
                    dst, rows_at(origin * size + (1 - zpar) * fetch, rest), mate,
                    fw_send.at[1, n, k - 1], fw_recv.at[1, n, k - 1],
                )

    for cp in small_copies:
        cp.wait()
    slot = lax.broadcasted_iota(jnp.int32, (S, 128), 0)
    lane = lax.broadcasted_iota(jnp.int32, (S, 128), 1)
    ftmp[...] = jnp.zeros_like(ftmp)
    ftmp[0:3, 0:owned] = (fbuf[...] > 0).astype(F32)
    for n in range(3):
        row = jnp.broadcast_to(ftmp[n : n + 1, :], (S, 128))
        column = jnp.sum(jnp.where(slot == lane, row, 0.0), axis=1, keepdims=True)
        masks[n] = jnp.broadcast_to(column, (S, 128))
    found = jnp.zeros((S, 128), F32)
    for w in range(pbuf.shape[1]):
        for q in range(pbuf.shape[2]):
            found = jnp.maximum(found, jnp.where(slot == pbuf[0, w, q], 1.0, 0.0))
    live[...] = found

    def cot_in(s, carry):
        v = cbuf[s].astype(F32)
        for h in range(2):
            cf[h, pl.ds(s * cs, opix), :] = v[:, h * 128 : (h + 1) * 128]
        return carry

    lax.fori_loop(0, owned, cot_in, 0)
    lv = live[...]

    def cot_rows(p, carry):
        for h in range(2):
            pair = [
                cf[h, pl.ds(2 * p + n, S, stride=cs), :] * lv for n in range(2)
            ]
            cotp[pl.ds(pl.multiple_of(p * 2 * S, 16), 2 * S), h * 128 : (h + 1) * 128] = (
                jnp.concatenate(pair, axis=0).astype(BF16)
            )
        return carry

    lax.fori_loop(0, opix // 2, cot_rows, 0)

    def split_rows(v):
        cores = [
            jnp.concatenate(
                [v[(2 * n + q) * cw : (2 * n + q + 1) * cw] for n in range(nz)], axis=0
            )
            for q in range(2)
        ]
        return cores

    def store_split(ref, v, lo, width):
        cores = split_rows(v)
        for q in range(2):
            at = core if q == 1 else 0
            at = (1 - core) if q == 1 else core
            ref[pl.ds(pl.multiple_of(at * half, 128), half), lo : lo + width] = cores[
                q
            ].astype(BF16)

    for n in range(2):
        rows = n * 2 * FS
        store_split(cot_t, cotp[rows : rows + 2 * FS, :].astype(F32).T, rows, 2 * FS)

    def tile_in(s, carry):
        v = tbuf[s].astype(F32)
        for h in range(2):
            xf[h, pl.ds(s * ts, cells), :] = v[:, h * 128 : (h + 1) * 128]
        return carry

    for cp, lo, count in tile_copies:
        cp.wait()
        lax.fori_loop(lo, lo + count, tile_in, 0)

    top, left, past = masks[0], masks[1], masks[2]

    def patch_rows(f, carry):
        hist = jnp.where(f >= 2, jnp.ones_like(past), past)
        hist_top, hist_left = hist * top, hist * left
        hist_both = hist_top * left
        for r in range(H):
            uses = [(r - 2 * i, i) for i in range(TR) if 0 <= r - 2 * i < 3]
            mask = hist_top if r == 0 else hist
            mask_left = hist_both if r == 0 else hist_left
            for h in range(2):
                cols = [
                    xf[h, pl.ds(f * (H * W) + r * W + c, S, stride=ts), :]
                    * (mask_left if c == 0 else mask)
                    for c in range(W)
                ]
                for kx in range(3):
                    for jp in range(TC // 2):
                        c = 4 * jp + kx
                        v = jnp.concatenate([cols[c], cols[c + 2]], axis=0).astype(BF16)
                        for ky, i in uses:
                            row = pl.ds(
                                pl.multiple_of(f * FS + (i * TC + 2 * jp) * S, 16), 2 * S
                            )
                            at = (3 * ky + kx) * C + h * 128
                            patches[row, at : at + 128] = v
        return carry

    steps = max(nb - 1, 1)
    cuts = [FR * n // steps for n in range(steps + 1)]
    for n in range(steps):
        if n + 1 < nb:
            relay(n + 1)
        if n > 1:
            relay_rest(n - 1)
        if cuts[n + 1] > cuts[n]:
            lax.fori_loop(cuts[n], cuts[n + 1], patch_rows, 0)
    for k in range(max(steps - 1, 1), nb):
        relay_rest(k)
    for cp in local:
        cp.wait()
    for cp in forwards.values():
        cp.wait_recv()

    def chunk(n):
        rows = n * 2 * FS
        pre = jnp.dot(patches[rows : rows + 2 * FS, :], wsp[...], preferred_element_type=F32)
        sig = 1.0 / (1.0 + jnp.exp(-pre))
        act[rows : rows + 2 * FS, :] = (pre * sig).astype(BF16)
        ga = None
        nt_dims = (((1,), (1,)), ((), ()))
        if n > 0:
            lo = (n - 1) * 2 * FS
            ga = lax.dot_general(
                cotp[lo : lo + 2 * FS, :], wtp[0:C, :], nt_dims, preferred_element_type=F32
            )
        if n < 2:
            g = lax.dot_general(
                cotp[rows : rows + 2 * FS, :], wtp[C : 2 * C, :], nt_dims,
                preferred_element_type=F32,
            )
            ga = g if ga is None else ga + g
        gp = ga * (sig * (1.0 + pre * (1.0 - sig)))
        store_split(grad_t, gp.T, rows, 2 * FS)

    for n in range(3):
        chunk(n)

    sp_lanes = nt * 128
    cut = (nt + 2) // 2
    spans = [(0, cut), (cut, nt)]
    bounds = [pl.ds(0, cut * 128), pl.ds(cut * 128, nl - cut * 128)]

    def section(h, k):
        to = bal_peer(k)
        lo, hi = spans[h]
        if hi > lo:
            sp_at = pl.multiple_of((to * rs) // 128 * 128 + lo * 128, 128)
            g = jnp.dot(
                grad_t[...], patches[:, pl.ds(sp_at, (hi - lo) * 128)],
                preferred_element_type=F32,
            )
            own[k - 1, :, lo * 128 : hi * 128] = g[0:half]
            s1[k - 1, :, lo * 128 : hi * 128] = g[half:].astype(BF16)
        if h == 1:
            tp_at = (to * rt) // 128 * 128
            tap = tp_at // C
            at = pl.multiple_of(tp_at - tap * C, 128)
            rows = pl.ds(pl.multiple_of((1 - tap) * 2 * FS, 16), TO * FS)
            g = jnp.dot(cot_t[...], act[rows, pl.ds(at, 128)], preferred_element_type=F32)
            own[k - 1, :, sp_lanes:] = g[0:half]
            s1[k - 1, :, sp_lanes:] = g[half:].astype(BF16)
        cp = pltpu.make_async_remote_copy(
            src_ref=s1.at[k - 1, :, bounds[h]], dst_ref=r1.at[k - 1, :, bounds[h]],
            send_sem=s1_send.at[h, k - 1], recv_sem=s1_recv.at[h, k - 1],
            device_id=(mate, b), device_id_type=MESH,
        )
        cp.start()
        first[h, k] = cp

    first, second, third = {}, {}, {}

    def pass_on(h, k):
        first[h, k].wait_recv()
        at = bounds[h]
        total = own[k - 1, :, at] + r1[k - 1, :, at].astype(F32)
        if k == nb:
            own[k - 1, :, at] = total
            return
        s2[k - 1, :, at] = total.astype(BF16)
        cp = pltpu.make_async_remote_copy(
            src_ref=s2.at[k - 1, :, at], dst_ref=r2.at[k - 1, :, at],
            send_sem=s2_send.at[h, k - 1], recv_sem=s2_recv.at[h, k - 1],
            device_id=(d, bal_peer(k)), device_id_type=MESH,
        )
        cp.start()
        second[h, k] = cp

    order = [(h, k) for h in range(2) for k in range(1, nb + 1)]
    lag = min(3, nb)
    for n, unit in enumerate(order):
        section(*unit)
        if n >= lag:
            pass_on(*order[n - lag])
    for unit in order[-lag:]:
        pass_on(*unit)

    def features(t0):
        rows = t0 * FS
        feat = jnp.dot(
            act[rows + 2 * FS : rows + 4 * FS, :], wtp[0:C, :], preferred_element_type=F32
        ) + jnp.dot(act[rows : rows + 2 * FS, :], wtp[C : 2 * C, :], preferred_element_type=F32)
        for p in range(2 * TR * TC):
            for h in range(2):
                v = feat[p * S : (p + 1) * S, h * 128 : (h + 1) * 128]
                cf[h, pl.ds(t0 * TR * TC + p, S, stride=cs), :] = v * lv

    def group_sum(h):
        at = bounds[h]
        total = own[nb - 1, :, at]
        for k in range(1, nb):
            second[h, k].wait_recv()
            total = total + r2[k - 1, :, at].astype(F32)
        for n in range(nz):
            part = total[n * cw : (n + 1) * cw]
            own3[n, :, at] = part
            if cwp > cw:
                part = jnp.concatenate(
                    [part, jnp.zeros((cwp - cw, part.shape[1]), F32)], axis=0
                )
            s3[n, :, at] = part.astype(BF16)
        for k in range(1, nz):
            to = z_peer(k)
            cp = pltpu.make_async_remote_copy(
                src_ref=s3.at[to, :, at], dst_ref=r3.at[k - 1, :, at],
                send_sem=s3_send.at[h, k - 1], recv_sem=s3_recv.at[h, k - 1],
                device_id=(2 * to + core, b), device_id_type=MESH,
            )
            cp.start()
            third[h, k] = cp

    features(0)
    features(2)
    group_sum(0)

    def feat_out(s, carry):
        cbuf[s] = jnp.concatenate(
            [cf[h, pl.ds(s * cs, opix), :] for h in range(2)], axis=1
        ).astype(BF16)
        return carry

    lax.fori_loop(0, owned, feat_out, 0)
    feat_copy = local_copy(cbuf, feat_ref, loc_sem.at[5])
    group_sum(1)
    for h in range(2):
        at = bounds[h]
        total = own3[z, :, at]
        for k in range(1, nz):
            third[h, k].wait_recv()
            total = total + r3[k - 1, :, at].astype(F32)[0:cw]
        grad_ref[:, at] = total * cfg["factor"]

    feat_copy.wait()
    for group in (gathers, relays, forwards, first, second, third):
        for cp in group.values():
            cp.wait_send()


def per_device(tiles, cotangent, halo_flags, send_plan, spatial_weight, temporal_weight):
    nd, nb = lax.axis_size("dp"), lax.axis_size("bal")
    owned, cells, C = tiles.shape
    opix = cotangent.shape[1]
    rs, rt = spatial_weight.shape[0], temporal_weight.shape[0]
    S = up(owned, 8)
    nt = max(-(-(rs * (n + 1)) // 128) - rs * n // 128 for n in range(nb))
    sp_lanes = nt * 128
    nl = sp_lanes + 128
    cw = C // nd
    cwp = up(cw, 16)
    nz = nd // 2
    half = C // 2
    n_parts = 4
    parts = [owned // n_parts + (n < owned % n_parts) for n in range(n_parts)]
    cfg = dict(
        nd=nd, nb=nb, owned=owned, C=C, S=S, rs=rs, rt=rt, nt=nt, nl=nl, cw=cw, cwp=cwp,
        parts=parts, factor=1.0 / math.sqrt(nd * nb * WORK_TILES),
    )
    M = FR * TR * TC * S
    K = TO * TR * TC * S
    vm = pltpu.VMEM
    dma = pltpu.SemaphoreType.DMA
    hbm = pl.BlockSpec(memory_space=pltpu.HBM)
    vspec = pl.BlockSpec(memory_space=pltpu.VMEM)
    scratch = [
        vm((owned, opix, C), BF16),
        vm((3, owned), jnp.int32),
        pltpu.SMEM(send_plan.shape, jnp.int32),
        vm((8, 128), F32),
        vm((owned, cells, C), BF16),
        vm((2, S * (cells + 1), 128), F32),
        vm((2, S * (opix + 1), 128), F32),
        vm((M, 9 * C), BF16),
        vm((K, C), BF16),
        vm((9 * C, C), BF16),
        vm((2 * C, C), BF16),
        vm((M, C), BF16),
        vm((8, 128), F32),
        vm((C, M), BF16),
        vm((C, K), BF16),
        vm((S, 128), F32),
        vm((3, S, 128), F32),
        vm((nb, half, nl), F32),
        vm((nb, half, nl), BF16),
        vm((nb, half, nl), BF16),
        vm((nb - 1, half, nl), BF16),
        vm((nb - 1, half, nl), BF16),
        vm((nz, cw, nl), F32),
        vm((nz, cwp, nl), BF16),
        vm((nz - 1, cwp, nl), BF16),
        dma((n_parts,)),
        dma((6,)),
        dma((2, nb - 1)), dma((2, nb - 1)), dma((2, nb - 1)), dma((2, nb - 1)),
        dma((2, 2, nb - 1)), dma((2, 2, nb - 1)),
        dma((2, nb)), dma((2, nb)),
        dma((2, nb - 1)), dma((2, nb - 1)),
        dma((2, nz - 1)), dma((2, nz - 1)),
    ]
    features, grads = pl.pallas_call(
        functools.partial(kernel, cfg),
        out_shape=(
            jax.ShapeDtypeStruct((owned, opix, C), BF16),
            jax.ShapeDtypeStruct((cw, nl), F32),
        ),
        in_specs=[hbm] * 6,
        out_specs=(hbm, vspec),
        scratch_shapes=scratch,
        compiler_params=pltpu.CompilerParams(
            collective_id=0, has_side_effects=True, vmem_limit_bytes=64 * 1024 * 1024 - 65536
        ),
    )(tiles, cotangent, halo_flags.T, send_plan, spatial_weight, temporal_weight)
    b = lax.axis_index("bal")
    sp = lax.dynamic_slice(grads, (0, lax.rem(b * rs, 128)), (cw, rs)).T
    tp = lax.dynamic_slice(grads, (0, sp_lanes + lax.rem(b * rt, 128)), (cw, rt)).T
    return (features, sp, tp)


def solution(mesh):
    in_specs = (
        P(("dp", "bal"), None, None),
        P(("dp", "bal"), None, None),
        P(("dp", "bal"), None),
        P(("dp", "bal"), None, None),
        P("bal", None),
        P("bal", None),
    )
    out_specs = (P(("dp", "bal"), None, None), P("bal", "dp"), P("bal", "dp"))
    return jax.shard_map(
        per_device, mesh=mesh, in_specs=in_specs, out_specs=out_specs, check_vma=False
    )
```

```python
import functools
import math

import jax
import jax.numpy as jnp
from jax import lax
from jax.experimental import pallas as pl
from jax.experimental.pallas import tpu as pltpu
from jax.sharding import PartitionSpec as P

FR, H, W = 6, 5, 9
TR, TC, TO = 2, 4, 4
WORK_TILES = 12
F32, BF16 = jnp.float32, jnp.bfloat16
MESH = pl.DeviceIdType.MESH
VMEM_LIMIT = 64 * 1024 * 1024 - 65536


def up(value, step):
    return (value + step - 1) // step * step


def kernel(
    cfg,
    tiles_ref, cot_ref, flags_ref, plan_ref, wsp_ref, wtp_ref,
    feat_ref, sp_ref, tp_ref,
    cbuf, fbuf, pbuf, ftmp, tbuf, xf, cf, patches, cotp, wsp, wtp, act, dact, grad_t, cot_t, live, masks,
    own, s1, r1, s2, r2, own3, s3, r3,
    tile_sem, loc_sem, ag_send, ag_recv, zr_send, zr_recv, fw_send, fw_recv,
    s1_send, s1_recv, s2_send, s2_recv, s3_send, s3_recv,
):
    nd, nb, owned, C = cfg["nd"], cfg["nb"], cfg["owned"], cfg["C"]
    S, rs, rt, nt, nl = cfg["S"], cfg["rs"], cfg["rt"], cfg["nt"], cfg["nl"]
    cw, cwp, parts = cfg["cw"], cfg["cwp"], cfg["parts"]
    nz = nd // 2
    cells, opix = FR * H * W, TO * TR * TC
    ts, cs = cells + 1, opix + 1
    FS = TR * TC * S
    half = C // 2

    d = lax.axis_index("dp")
    b = lax.axis_index("bal")
    core = lax.rem(d, 2)
    z = d // 2
    mate = d + 1 - 2 * core

    def bal_peer(k):
        return lax.rem(b + k, nb)

    def z_peer(k):
        return lax.rem(z + k, nz)

    def local_copy(src, dst, sem):
        cp = pltpu.make_async_copy(src, dst, sem)
        cp.start()
        return cp

    barrier = pltpu.get_barrier_semaphore()
    pl.semaphore_signal(barrier, inc=1, device_id=(mate, b), device_id_type=MESH)
    for k in range(1, nb):
        pl.semaphore_signal(barrier, inc=1, device_id=(d, bal_peer(k)), device_id_type=MESH)
    for k in range(1, nz):
        pl.semaphore_signal(
            barrier, inc=1, device_id=(2 * z_peer(k) + core, b), device_id_type=MESH
        )

    small_copies = [
        local_copy(flags_ref, fbuf, loc_sem.at[2]),
        local_copy(plan_ref, pbuf, loc_sem.at[3]),
        local_copy(cot_ref, cbuf, loc_sem.at[4]),
    ]
    tile_copies = []
    lo = 0
    for n, count in enumerate(parts):
        part = pl.ds(lo, count)
        cp = local_copy(tiles_ref.at[part], tbuf.at[part], tile_sem.at[n])
        tile_copies.append((cp, lo, count))
        lo += count
    my_sp = pl.ds(pl.multiple_of(b * rs, 16), rs)
    my_tp = pl.ds(pl.multiple_of(b * rt, 16), rt)
    local = [
        local_copy(wsp_ref, wsp.at[my_sp], loc_sem.at[0]),
        local_copy(wtp_ref, wtp.at[my_tp], loc_sem.at[1]),
    ]

    if S > owned:
        for h in range(2):
            cf[h, owned * cs : S * cs, :] = jnp.zeros(((S - owned) * cs, 128), F32)
            xf[h, owned * ts : S * ts, :] = jnp.zeros(((S - owned) * ts, 128), F32)

    pl.semaphore_wait(barrier, nb + nz - 1)

    lanes = pl.ds(pl.multiple_of(core * half, 128), half)
    zpar = lax.rem(z, 2)
    zmate = 2 * (z + 1 - 2 * zpar) + core
    weights = []
    for src, dst, size in ((wsp_ref, wsp, rs), (wtp_ref, wtp, rt)):
        units = size // 16
        fetch = units if nz % 2 else max((units + 1) // 2, round(0.6 * units))
        weights.append((src, dst, size, fetch * 16, (units - fetch) * 16))

    def rows_at(start, count):
        return pl.ds(pl.multiple_of(start, 16), count)

    gathers, relays, forwards = {}, {}, {}
    for k in range(1, nb):
        for n, (src, dst, size, fetch, rest) in enumerate(weights):
            cp = pltpu.make_async_remote_copy(
                src_ref=src.at[rows_at(zpar * rest, fetch), lanes],
                dst_ref=dst.at[rows_at(b * size + zpar * rest, fetch), lanes],
                send_sem=ag_send.at[n, k - 1],
                recv_sem=ag_recv.at[n, k - 1],
                device_id=(d, bal_peer(k)),
                device_id_type=MESH,
            )
            cp.start()
            gathers[n, k] = cp

    def push(ref, rows, to, send, recv):
        cp = pltpu.make_async_remote_copy(
            src_ref=ref.at[rows, lanes], dst_ref=ref.at[rows, lanes],
            send_sem=send, recv_sem=recv, device_id=(to, b), device_id_type=MESH,
        )
        cp.start()
        return cp

    def relay(k):
        origin = lax.rem(b + nb - k, nb)
        for n, (src, dst, size, fetch, rest) in enumerate(weights):
            gathers[n, k].wait_recv()
            if rest:
                relays[n, k] = push(
                    dst, rows_at(origin * size + zpar * fetch, rest), zmate,
                    zr_send.at[n, k - 1], zr_recv.at[n, k - 1],
                )
            forwards[0, n, k] = push(
                dst, rows_at(origin * size + zpar * rest, fetch), mate,
                fw_send.at[0, n, k - 1], fw_recv.at[0, n, k - 1],
            )

    def relay_rest(k):
        origin = lax.rem(b + nb - k, nb)
        for n, (src, dst, size, fetch, rest) in enumerate(weights):
            if rest:
                relays[n, k].wait_recv()
                forwards[1, n, k] = push(
                    dst, rows_at(origin * size + (1 - zpar) * fetch, rest), mate,
                    fw_send.at[1, n, k - 1], fw_recv.at[1, n, k - 1],
                )

    for cp in small_copies:
        cp.wait()
    slot = lax.broadcasted_iota(jnp.int32, (S, 128), 0)
    lane = lax.broadcasted_iota(jnp.int32, (S, 128), 1)
    ftmp[...] = jnp.zeros_like(ftmp)
    ftmp[0:3, 0:owned] = (fbuf[...] > 0).astype(F32)
    for n in range(3):
        row = jnp.broadcast_to(ftmp[n : n + 1, :], (S, 128))
        column = jnp.sum(jnp.where(slot == lane, row, 0.0), axis=1, keepdims=True)
        masks[n] = jnp.broadcast_to(column, (S, 128))
    found = jnp.zeros((S, 128), F32)
    for w in range(pbuf.shape[1]):
        for q in range(pbuf.shape[2]):
            found = jnp.maximum(found, jnp.where(slot == pbuf[0, w, q], 1.0, 0.0))
    live[...] = found

    def cot_in(s, carry):
        v = cbuf[s].astype(F32)
        for h in range(2):
            cf[h, pl.ds(s * cs, opix), :] = v[:, h * 128 : (h + 1) * 128]
        return carry

    lax.fori_loop(0, owned, cot_in, 0)
    lv = live[...]

    def cot_rows(p, carry):
        for h in range(2):
            pair = [
                cf[h, pl.ds(2 * p + n, S, stride=cs), :] * lv for n in range(2)
            ]
            cotp[pl.ds(pl.multiple_of(p * 2 * S, 16), 2 * S), h * 128 : (h + 1) * 128] = (
                jnp.concatenate(pair, axis=0).astype(BF16)
            )
        return carry

    lax.fori_loop(0, opix // 2, cot_rows, 0)

    def split_rows(v):
        cores = [
            jnp.concatenate(
                [v[(2 * n + q) * cw : (2 * n + q + 1) * cw] for n in range(nz)], axis=0
            )
            for q in range(2)
        ]
        return cores

    def store_split(ref, v, lo, width):
        cores = split_rows(v)
        for q in range(2):
            at = core if q == 1 else 0
            at = (1 - core) if q == 1 else core
            ref[pl.ds(pl.multiple_of(at * half, 128), half), lo : lo + width] = cores[
                q
            ].astype(BF16)

    for n in range(2):
        rows = n * 2 * FS
        store_split(cot_t, cotp[rows : rows + 2 * FS, :].astype(F32).T, rows, 2 * FS)

    def tile_in(s, carry):
        v = tbuf[s].astype(F32)
        for h in range(2):
            xf[h, pl.ds(s * ts, cells), :] = v[:, h * 128 : (h + 1) * 128]
        return carry

    for cp, lo, count in tile_copies:
        cp.wait()
        lax.fori_loop(lo, lo + count, tile_in, 0)

    top, left, past = masks[0], masks[1], masks[2]

    def patch_rows(f, carry):
        hist = jnp.where(f >= 2, jnp.ones_like(past), past)
        hist_top, hist_left = hist * top, hist * left
        hist_both = hist_top * left
        for r in range(H):
            uses = [(r - 2 * i, i) for i in range(TR) if 0 <= r - 2 * i < 3]
            mask = hist_top if r == 0 else hist
            mask_left = hist_both if r == 0 else hist_left
            for h in range(2):
                cols = [
                    xf[h, pl.ds(f * (H * W) + r * W + c, S, stride=ts), :]
                    * (mask_left if c == 0 else mask)
                    for c in range(W)
                ]
                for kx in range(3):
                    for jp in range(TC // 2):
                        c = 4 * jp + kx
                        v = jnp.concatenate([cols[c], cols[c + 2]], axis=0).astype(BF16)
                        for ky, i in uses:
                            row = pl.ds(
                                pl.multiple_of(f * FS + (i * TC + 2 * jp) * S, 16), 2 * S
                            )
                            at = (3 * ky + kx) * C + h * 128
                            patches[row, at : at + 128] = v
        return carry

    steps = max(nb - 1, 1)
    cuts = [FR * n // steps for n in range(steps + 1)]
    for n in range(steps):
        if n + 1 < nb:
            relay(n + 1)
        if n > 1:
            relay_rest(n - 1)
        if cuts[n + 1] > cuts[n]:
            lax.fori_loop(cuts[n], cuts[n + 1], patch_rows, 0)
    for k in range(max(steps - 1, 1), nb):
        relay_rest(k)
    for cp in local:
        cp.wait()
    for cp in forwards.values():
        cp.wait_recv()

    def chunk(n):
        rows = n * 2 * FS
        pre = jnp.dot(patches[rows : rows + 2 * FS, :], wsp[...], preferred_element_type=F32)
        sig = 1.0 / (1.0 + jnp.exp(-pre))
        act[rows : rows + 2 * FS, :] = (pre * sig).astype(BF16)
        ga = None
        nt_dims = (((1,), (1,)), ((), ()))
        if n > 0:
            lo = (n - 1) * 2 * FS
            ga = lax.dot_general(
                cotp[lo : lo + 2 * FS, :], wtp[0:C, :], nt_dims, preferred_element_type=F32
            )
        if n < 2:
            g = lax.dot_general(
                cotp[rows : rows + 2 * FS, :], wtp[C : 2 * C, :], nt_dims,
                preferred_element_type=F32,
            )
            ga = g if ga is None else ga + g
        gp = ga * (sig * (1.0 + pre * (1.0 - sig)))
        store_split(grad_t, gp.T, rows, 2 * FS)

    for n in range(3):
        chunk(n)

    sp_lanes = nt * 128
    cut = (nt + 2) // 2
    spans = [(0, cut), (cut, nt)]
    bounds = [pl.ds(0, cut * 128), pl.ds(cut * 128, nl - cut * 128)]

    def section(h, k):
        to = bal_peer(k)
        lo, hi = spans[h]
        if hi > lo:
            sp_at = pl.multiple_of((to * rs) // 128 * 128 + lo * 128, 128)
            g = jnp.dot(
                grad_t[...], patches[:, pl.ds(sp_at, (hi - lo) * 128)],
                preferred_element_type=F32,
            )
            own[k - 1, :, lo * 128 : hi * 128] = g[0:half]
            s1[k - 1, :, lo * 128 : hi * 128] = g[half:].astype(BF16)
        if h == 1:
            tp_at = (to * rt) // 128 * 128
            tap = tp_at // C
            at = pl.multiple_of(tp_at - tap * C, 128)
            rows = pl.ds(pl.multiple_of((1 - tap) * 2 * FS, 16), TO * FS)
            g = jnp.dot(cot_t[...], act[rows, pl.ds(at, 128)], preferred_element_type=F32)
            own[k - 1, :, sp_lanes:] = g[0:half]
            s1[k - 1, :, sp_lanes:] = g[half:].astype(BF16)
        cp = pltpu.make_async_remote_copy(
            src_ref=s1.at[k - 1, :, bounds[h]], dst_ref=r1.at[k - 1, :, bounds[h]],
            send_sem=s1_send.at[h, k - 1], recv_sem=s1_recv.at[h, k - 1],
            device_id=(mate, b), device_id_type=MESH,
        )
        cp.start()
        first[h, k] = cp

    first, second, third = {}, {}, {}

    def pass_on(h, k):
        first[h, k].wait_recv()
        at = bounds[h]
        total = own[k - 1, :, at] + r1[k - 1, :, at].astype(F32)
        if k == nb:
            own[k - 1, :, at] = total
            return
        s2[k - 1, :, at] = total.astype(BF16)
        cp = pltpu.make_async_remote_copy(
            src_ref=s2.at[k - 1, :, at], dst_ref=r2.at[k - 1, :, at],
            send_sem=s2_send.at[h, k - 1], recv_sem=s2_recv.at[h, k - 1],
            device_id=(d, bal_peer(k)), device_id_type=MESH,
        )
        cp.start()
        second[h, k] = cp

    order = [(h, k) for h in range(2) for k in range(1, nb + 1)]
    lag = min(3, nb)
    for n, unit in enumerate(order):
        section(*unit)
        if n >= lag:
            pass_on(*order[n - lag])
    for unit in order[-lag:]:
        pass_on(*unit)

    def features(t0):
        rows = t0 * FS
        feat = jnp.dot(
            act[rows + 2 * FS : rows + 4 * FS, :], wtp[0:C, :], preferred_element_type=F32
        ) + jnp.dot(act[rows : rows + 2 * FS, :], wtp[C : 2 * C, :], preferred_element_type=F32)
        for p in range(2 * TR * TC):
            for h in range(2):
                v = feat[p * S : (p + 1) * S, h * 128 : (h + 1) * 128]
                cf[h, pl.ds(t0 * TR * TC + p, S, stride=cs), :] = v * lv

    def group_sum(h):
        at = bounds[h]
        total = own[nb - 1, :, at]
        for k in range(1, nb):
            second[h, k].wait_recv()
            total = total + r2[k - 1, :, at].astype(F32)
        for n in range(nz):
            part = total[n * cw : (n + 1) * cw]
            own3[n, :, at] = part
            if cwp > cw:
                part = jnp.concatenate(
                    [part, jnp.zeros((cwp - cw, part.shape[1]), F32)], axis=0
                )
            s3[n, :, at] = part.astype(BF16)
        for k in range(1, nz):
            to = z_peer(k)
            cp = pltpu.make_async_remote_copy(
                src_ref=s3.at[to, :, at], dst_ref=r3.at[k - 1, :, at],
                send_sem=s3_send.at[h, k - 1], recv_sem=s3_recv.at[h, k - 1],
                device_id=(2 * to + core, b), device_id_type=MESH,
            )
            cp.start()
            third[h, k] = cp

    features(0)
    features(2)
    group_sum(0)

    def feat_out(s, carry):
        cbuf[s] = jnp.concatenate(
            [cf[h, pl.ds(s * cs, opix), :] for h in range(2)], axis=1
        ).astype(BF16)
        return carry

    lax.fori_loop(0, owned, feat_out, 0)
    feat_copy = local_copy(cbuf, feat_ref, loc_sem.at[5])
    group_sum(1)
    sums = []
    for h in range(2):
        at = bounds[h]
        total = own3[z, :, at]
        for k in range(1, nz):
            third[h, k].wait_recv()
            total = total + r3[k - 1, :, at].astype(F32)[0:cw]
        sums.append(total * cfg["factor"])
    total = jnp.concatenate(sums, axis=1)
    sp_sum, tp_sum = total[:, :sp_lanes], total[:, sp_lanes:]
    if rs % 128:
        sp_sum = pltpu.roll(sp_sum, lax.rem(sp_lanes - lax.rem(b * rs, 128), sp_lanes), 1)
    if rt % 128:
        tp_sum = pltpu.roll(tp_sum, lax.rem(128 - lax.rem(b * rt, 128), 128), 1)
    sp_ref[...] = sp_sum[:, :rs]
    tp_ref[...] = tp_sum[:, :rt]

    feat_copy.wait()
    for group in (gathers, relays, forwards, first, second, third):
        for cp in group.values():
            cp.wait_send()


def hand_out(feat_in, sp_in, tp_in, feat_out, sp_out, tp_out, sem):
    copies = [
        pltpu.make_async_copy(src, dst, sem.at[n])
        for n, (src, dst) in enumerate(
            ((feat_in, feat_out), (sp_in, sp_out), (tp_in, tp_out))
        )
    ]
    for cp in copies:
        cp.start()
    for cp in copies:
        cp.wait()


def per_device(tiles, cotangent, halo_flags, send_plan, spatial_weight, temporal_weight):
    nd, nb = lax.axis_size("dp"), lax.axis_size("bal")
    owned, cells, C = tiles.shape
    opix = cotangent.shape[1]
    rs, rt = spatial_weight.shape[0], temporal_weight.shape[0]
    S = up(owned, 8)
    nt = max(-(-(rs * (n + 1)) // 128) - rs * n // 128 for n in range(nb))
    sp_lanes = nt * 128
    nl = sp_lanes + 128
    cw = C // nd
    cwp = up(cw, 16)
    nz = nd // 2
    half = C // 2
    n_parts = 4
    parts = [owned // n_parts + (n < owned % n_parts) for n in range(n_parts)]
    cfg = dict(
        nd=nd, nb=nb, owned=owned, C=C, S=S, rs=rs, rt=rt, nt=nt, nl=nl, cw=cw, cwp=cwp,
        parts=parts, factor=1.0 / math.sqrt(nd * nb * WORK_TILES),
    )
    M = FR * TR * TC * S
    K = TO * TR * TC * S
    vm = pltpu.VMEM
    dma = pltpu.SemaphoreType.DMA
    hbm = pl.BlockSpec(memory_space=pltpu.HBM)
    vspec = pl.BlockSpec(memory_space=pltpu.VMEM)
    scratch = [
        vm((owned, opix, C), BF16),
        vm((3, owned), jnp.int32),
        pltpu.SMEM(send_plan.shape, jnp.int32),
        vm((8, 128), F32),
        vm((owned, cells, C), BF16),
        vm((2, S * (cells + 1), 128), F32),
        vm((2, S * (opix + 1), 128), F32),
        vm((M, 9 * C), BF16),
        vm((K, C), BF16),
        vm((9 * C, C), BF16),
        vm((2 * C, C), BF16),
        vm((M, C), BF16),
        vm((8, 128), F32),
        vm((C, M), BF16),
        vm((C, K), BF16),
        vm((S, 128), F32),
        vm((3, S, 128), F32),
        vm((nb, half, nl), F32),
        vm((nb, half, nl), BF16),
        vm((nb, half, nl), BF16),
        vm((nb - 1, half, nl), BF16),
        vm((nb - 1, half, nl), BF16),
        vm((nz, cw, nl), F32),
        vm((nz, cwp, nl), BF16),
        vm((nz - 1, cwp, nl), BF16),
        dma((n_parts,)),
        dma((6,)),
        dma((2, nb - 1)), dma((2, nb - 1)), dma((2, nb - 1)), dma((2, nb - 1)),
        dma((2, 2, nb - 1)), dma((2, 2, nb - 1)),
        dma((2, nb)), dma((2, nb)),
        dma((2, nb - 1)), dma((2, nb - 1)),
        dma((2, nz - 1)), dma((2, nz - 1)),
    ]
    shapes = (
        jax.ShapeDtypeStruct((owned, opix, C), BF16),
        jax.ShapeDtypeStruct((cw, rs), F32),
        jax.ShapeDtypeStruct((cw, rt), F32),
    )
    results = pl.pallas_call(
        functools.partial(kernel, cfg),
        out_shape=shapes,
        in_specs=[hbm] * 6,
        out_specs=(hbm, vspec, vspec),
        scratch_shapes=scratch,
        compiler_params=pltpu.CompilerParams(
            collective_id=0, has_side_effects=True, vmem_limit_bytes=VMEM_LIMIT
        ),
    )(tiles, cotangent, halo_flags.T, send_plan, spatial_weight, temporal_weight)
    features, sp, tp = pl.pallas_call(
        hand_out,
        out_shape=shapes,
        in_specs=[hbm] * 3,
        out_specs=(hbm, hbm, hbm),
        scratch_shapes=[dma((3,))],
        compiler_params=pltpu.CompilerParams(vmem_limit_bytes=VMEM_LIMIT),
    )(*results)
    return (features, sp.T, tp.T)


def solution(mesh):
    in_specs = (
        P(("dp", "bal"), None, None),
        P(("dp", "bal"), None, None),
        P(("dp", "bal"), None),
        P(("dp", "bal"), None, None),
        P("bal", None),
        P("bal", None),
    )
    out_specs = (P(("dp", "bal"), None, None), P("bal", "dp"), P("bal", "dp"))
    return jax.shard_map(
        per_device, mesh=mesh, in_specs=in_specs, out_specs=out_specs, check_vma=False
    )
```

```python
import functools
import math

import jax
import jax.numpy as jnp
from jax import lax
from jax.experimental import pallas as pl
from jax.experimental.pallas import tpu as pltpu
from jax.sharding import PartitionSpec as P

FR, H, W = 6, 5, 9
TR, TC, TO = 2, 4, 4
WORK_TILES = 12
F32, BF16 = jnp.float32, jnp.bfloat16
MESH = pl.DeviceIdType.MESH
VMEM_LIMIT = 64 * 1024 * 1024 - 65536


def up(value, step):
    return (value + step - 1) // step * step


def kernel(
    cfg,
    tiles_ref, cot_ref, flags_ref, plan_ref, wsp_ref, wtp_ref,
    feat_ref, sp_ref, tp_ref,
    cbuf, fbuf, pbuf, ftmp, tbuf, xf, cf, patches, cotp, wsp, wtp, act, dact, grad_t, cot_t, live, masks,
    own, s1, r1, s2, r2, own3, s3, r3,
    tile_sem, loc_sem, ag_send, ag_recv, zr_send, zr_recv, fw_send, fw_recv,
    s1_send, s1_recv, s2_send, s2_recv, s3_send, s3_recv,
):
    nd, nb, owned, C = cfg["nd"], cfg["nb"], cfg["owned"], cfg["C"]
    S, rs, rt, nt, nl = cfg["S"], cfg["rs"], cfg["rt"], cfg["nt"], cfg["nl"]
    cw, cwp, parts = cfg["cw"], cfg["cwp"], cfg["parts"]
    nz = nd // 2
    cells, opix = FR * H * W, TO * TR * TC
    ts, cs = cells + 1, opix + 1
    FS = TR * TC * S
    half = C // 2

    d = lax.axis_index("dp")
    b = lax.axis_index("bal")
    core = lax.rem(d, 2)
    z = d // 2
    mate = d + 1 - 2 * core

    def bal_peer(k):
        return lax.rem(b + k, nb)

    def z_peer(k):
        return lax.rem(z + k, nz)

    def local_copy(src, dst, sem):
        cp = pltpu.make_async_copy(src, dst, sem)
        cp.start()
        return cp

    barrier = pltpu.get_barrier_semaphore()
    pl.semaphore_signal(barrier, inc=1, device_id=(mate, b), device_id_type=MESH)
    for k in range(1, nb):
        pl.semaphore_signal(barrier, inc=1, device_id=(d, bal_peer(k)), device_id_type=MESH)
    for k in range(1, nz):
        pl.semaphore_signal(
            barrier, inc=1, device_id=(2 * z_peer(k) + core, b), device_id_type=MESH
        )

    my_sp = pl.ds(pl.multiple_of(b * rs, 16), rs)
    my_tp = pl.ds(pl.multiple_of(b * rt, 16), rt)
    local = [
        local_copy(wsp_ref, wsp.at[my_sp], loc_sem.at[0]),
        local_copy(wtp_ref, wtp.at[my_tp], loc_sem.at[1]),
    ]
    small_copies = [
        local_copy(flags_ref, fbuf, loc_sem.at[2]),
        local_copy(plan_ref, pbuf, loc_sem.at[3]),
        local_copy(cot_ref, cbuf, loc_sem.at[4]),
    ]
    tile_copies = []
    lo = 0
    for n, count in enumerate(parts):
        part = pl.ds(lo, count)
        cp = local_copy(tiles_ref.at[part], tbuf.at[part], tile_sem.at[n])
        tile_copies.append((cp, lo, count))
        lo += count
    if S > owned:
        for h in range(2):
            cf[h, owned * cs : S * cs, :] = jnp.zeros(((S - owned) * cs, 128), F32)
            xf[h, owned * ts : S * ts, :] = jnp.zeros(((S - owned) * ts, 128), F32)

    for cp in local:
        cp.wait()
    pl.semaphore_wait(barrier, nb + nz - 1)

    lanes = pl.ds(pl.multiple_of(core * half, 128), half)
    zpar = lax.rem(z, 2)
    zmate = 2 * (z + 1 - 2 * zpar) + core
    weights = []
    for src, dst, size in ((wsp_ref, wsp, rs), (wtp_ref, wtp, rt)):
        units = size // 16
        fetch = units if nz % 2 else max((units + 1) // 2, round(0.6 * units))
        weights.append((src, dst, size, fetch * 16, (units - fetch) * 16))

    def rows_at(start, count):
        return pl.ds(pl.multiple_of(start, 16), count)

    gathers, relays, forwards = {}, {}, {}
    for k in range(1, nb):
        for n, (src, dst, size, fetch, rest) in enumerate(weights):
            cp = pltpu.make_async_remote_copy(
                src_ref=dst.at[rows_at(b * size + zpar * rest, fetch), lanes],
                dst_ref=dst.at[rows_at(b * size + zpar * rest, fetch), lanes],
                send_sem=ag_send.at[n, k - 1],
                recv_sem=ag_recv.at[n, k - 1],
                device_id=(d, bal_peer(k)),
                device_id_type=MESH,
            )
            cp.start()
            gathers[n, k] = cp

    def push(ref, rows, to, send, recv):
        cp = pltpu.make_async_remote_copy(
            src_ref=ref.at[rows, lanes], dst_ref=ref.at[rows, lanes],
            send_sem=send, recv_sem=recv, device_id=(to, b), device_id_type=MESH,
        )
        cp.start()
        return cp

    def relay(k):
        origin = lax.rem(b + nb - k, nb)
        for n, (src, dst, size, fetch, rest) in enumerate(weights):
            gathers[n, k].wait_recv()
            if rest:
                relays[n, k] = push(
                    dst, rows_at(origin * size + zpar * fetch, rest), zmate,
                    zr_send.at[n, k - 1], zr_recv.at[n, k - 1],
                )
            forwards[0, n, k] = push(
                dst, rows_at(origin * size + zpar * rest, fetch), mate,
                fw_send.at[0, n, k - 1], fw_recv.at[0, n, k - 1],
            )

    def relay_rest(k):
        origin = lax.rem(b + nb - k, nb)
        for n, (src, dst, size, fetch, rest) in enumerate(weights):
            if rest:
                relays[n, k].wait_recv()
                forwards[1, n, k] = push(
                    dst, rows_at(origin * size + (1 - zpar) * fetch, rest), mate,
                    fw_send.at[1, n, k - 1], fw_recv.at[1, n, k - 1],
                )

    for cp in small_copies:
        cp.wait()
    slot = lax.broadcasted_iota(jnp.int32, (S, 128), 0)
    lane = lax.broadcasted_iota(jnp.int32, (S, 128), 1)
    ftmp[...] = jnp.zeros_like(ftmp)
    ftmp[0:3, 0:owned] = (fbuf[...] > 0).astype(F32)
    for n in range(3):
        row = jnp.broadcast_to(ftmp[n : n + 1, :], (S, 128))
        column = jnp.sum(jnp.where(slot == lane, row, 0.0), axis=1, keepdims=True)
        masks[n] = jnp.broadcast_to(column, (S, 128))
    found = jnp.zeros((S, 128), F32)
    for w in range(pbuf.shape[1]):
        for q in range(pbuf.shape[2]):
            found = jnp.maximum(found, jnp.where(slot == pbuf[0, w, q], 1.0, 0.0))
    live[...] = found

    def cot_in(s, carry):
        v = cbuf[s].astype(F32)
        for h in range(2):
            cf[h, pl.ds(s * cs, opix), :] = v[:, h * 128 : (h + 1) * 128]
        return carry

    lax.fori_loop(0, owned, cot_in, 0)
    lv = live[...]

    def cot_rows(p, carry):
        for h in range(2):
            pair = [
                cf[h, pl.ds(2 * p + n, S, stride=cs), :] * lv for n in range(2)
            ]
            cotp[pl.ds(pl.multiple_of(p * 2 * S, 16), 2 * S), h * 128 : (h + 1) * 128] = (
                jnp.concatenate(pair, axis=0).astype(BF16)
            )
        return carry

    lax.fori_loop(0, opix // 2, cot_rows, 0)

    def split_rows(v):
        cores = [
            jnp.concatenate(
                [v[(2 * n + q) * cw : (2 * n + q + 1) * cw] for n in range(nz)], axis=0
            )
            for q in range(2)
        ]
        return cores

    def store_split(ref, v, lo, width):
        cores = split_rows(v)
        for q in range(2):
            at = core if q == 1 else 0
            at = (1 - core) if q == 1 else core
            ref[pl.ds(pl.multiple_of(at * half, 128), half), lo : lo + width] = cores[
                q
            ].astype(BF16)

    for n in range(2):
        rows = n * 2 * FS
        store_split(cot_t, cotp[rows : rows + 2 * FS, :].astype(F32).T, rows, 2 * FS)

    def tile_in(s, carry):
        v = tbuf[s].astype(F32)
        for h in range(2):
            xf[h, pl.ds(s * ts, cells), :] = v[:, h * 128 : (h + 1) * 128]
        return carry

    for cp, lo, count in tile_copies:
        cp.wait()
        lax.fori_loop(lo, lo + count, tile_in, 0)

    top, left, past = masks[0], masks[1], masks[2]

    def patch_rows(f, carry):
        hist = jnp.where(f >= 2, jnp.ones_like(past), past)
        hist_top, hist_left = hist * top, hist * left
        hist_both = hist_top * left
        for r in range(H):
            uses = [(r - 2 * i, i) for i in range(TR) if 0 <= r - 2 * i < 3]
            mask = hist_top if r == 0 else hist
            mask_left = hist_both if r == 0 else hist_left
            for h in range(2):
                cols = [
                    xf[h, pl.ds(f * (H * W) + r * W + c, S, stride=ts), :]
                    * (mask_left if c == 0 else mask)
                    for c in range(W)
                ]
                for kx in range(3):
                    for jp in range(TC // 2):
                        c = 4 * jp + kx
                        v = jnp.concatenate([cols[c], cols[c + 2]], axis=0).astype(BF16)
                        for ky, i in uses:
                            row = pl.ds(
                                pl.multiple_of(f * FS + (i * TC + 2 * jp) * S, 16), 2 * S
                            )
                            at = (3 * ky + kx) * C + h * 128
                            patches[row, at : at + 128] = v
        return carry

    steps = max(nb - 1, 1)
    cuts = [FR * n // steps for n in range(steps + 1)]
    for n in range(steps):
        if n + 1 < nb:
            relay(n + 1)
        if n > 1:
            relay_rest(n - 1)
        if cuts[n + 1] > cuts[n]:
            lax.fori_loop(cuts[n], cuts[n + 1], patch_rows, 0)
    for k in range(max(steps - 1, 1), nb):
        relay_rest(k)
    for cp in forwards.values():
        cp.wait_recv()

    def chunk(n):
        rows = n * 2 * FS
        pre = jnp.dot(patches[rows : rows + 2 * FS, :], wsp[...], preferred_element_type=F32)
        sig = 1.0 / (1.0 + jnp.exp(-pre))
        act[rows : rows + 2 * FS, :] = (pre * sig).astype(BF16)
        ga = None
        nt_dims = (((1,), (1,)), ((), ()))
        if n > 0:
            lo = (n - 1) * 2 * FS
            ga = lax.dot_general(
                cotp[lo : lo + 2 * FS, :], wtp[0:C, :], nt_dims, preferred_element_type=F32
            )
        if n < 2:
            g = lax.dot_general(
                cotp[rows : rows + 2 * FS, :], wtp[C : 2 * C, :], nt_dims,
                preferred_element_type=F32,
            )
            ga = g if ga is None else ga + g
        gp = ga * (sig * (1.0 + pre * (1.0 - sig)))
        store_split(grad_t, gp.T, rows, 2 * FS)

    for n in range(3):
        chunk(n)

    sp_lanes = nt * 128
    cut = (nt + 2) // 2
    spans = [(0, cut), (cut, nt)]
    bounds = [pl.ds(0, cut * 128), pl.ds(cut * 128, nl - cut * 128)]

    def section(h, k):
        to = bal_peer(k)
        lo, hi = spans[h]
        if hi > lo:
            sp_at = pl.multiple_of((to * rs) // 128 * 128 + lo * 128, 128)
            g = jnp.dot(
                grad_t[...], patches[:, pl.ds(sp_at, (hi - lo) * 128)],
                preferred_element_type=F32,
            )
            own[k - 1, :, lo * 128 : hi * 128] = g[0:half]
            s1[k - 1, :, lo * 128 : hi * 128] = g[half:].astype(BF16)
        if h == 1:
            tp_at = (to * rt) // 128 * 128
            tap = tp_at // C
            at = pl.multiple_of(tp_at - tap * C, 128)
            rows = pl.ds(pl.multiple_of((1 - tap) * 2 * FS, 16), TO * FS)
            g = jnp.dot(cot_t[...], act[rows, pl.ds(at, 128)], preferred_element_type=F32)
            own[k - 1, :, sp_lanes:] = g[0:half]
            s1[k - 1, :, sp_lanes:] = g[half:].astype(BF16)
        cp = pltpu.make_async_remote_copy(
            src_ref=s1.at[k - 1, :, bounds[h]], dst_ref=r1.at[k - 1, :, bounds[h]],
            send_sem=s1_send.at[h, k - 1], recv_sem=s1_recv.at[h, k - 1],
            device_id=(mate, b), device_id_type=MESH,
        )
        cp.start()
        first[h, k] = cp

    first, second, third = {}, {}, {}

    def pass_on(h, k):
        first[h, k].wait_recv()
        at = bounds[h]
        total = own[k - 1, :, at] + r1[k - 1, :, at].astype(F32)
        if k == nb:
            own[k - 1, :, at] = total
            return
        s2[k - 1, :, at] = total.astype(BF16)
        cp = pltpu.make_async_remote_copy(
            src_ref=s2.at[k - 1, :, at], dst_ref=r2.at[k - 1, :, at],
            send_sem=s2_send.at[h, k - 1], recv_sem=s2_recv.at[h, k - 1],
            device_id=(d, bal_peer(k)), device_id_type=MESH,
        )
        cp.start()
        second[h, k] = cp

    order = [(h, k) for h in range(2) for k in range(1, nb + 1)]
    lag = min(3, nb)
    for n, unit in enumerate(order):
        section(*unit)
        if n >= lag:
            pass_on(*order[n - lag])
    for unit in order[-lag:]:
        pass_on(*unit)

    def features(t0):
        rows = t0 * FS
        feat = jnp.dot(
            act[rows + 2 * FS : rows + 4 * FS, :], wtp[0:C, :], preferred_element_type=F32
        ) + jnp.dot(act[rows : rows + 2 * FS, :], wtp[C : 2 * C, :], preferred_element_type=F32)
        for p in range(2 * TR * TC):
            for h in range(2):
                v = feat[p * S : (p + 1) * S, h * 128 : (h + 1) * 128]
                cf[h, pl.ds(t0 * TR * TC + p, S, stride=cs), :] = v * lv

    def group_sum(h):
        at = bounds[h]
        total = own[nb - 1, :, at]
        for k in range(1, nb):
            second[h, k].wait_recv()
            total = total + r2[k - 1, :, at].astype(F32)
        for n in range(nz):
            part = total[n * cw : (n + 1) * cw]
            own3[n, :, at] = part
            if cwp > cw:
                part = jnp.concatenate(
                    [part, jnp.zeros((cwp - cw, part.shape[1]), F32)], axis=0
                )
            s3[n, :, at] = part.astype(BF16)
        for k in range(1, nz):
            to = z_peer(k)
            cp = pltpu.make_async_remote_copy(
                src_ref=s3.at[to, :, at], dst_ref=r3.at[k - 1, :, at],
                send_sem=s3_send.at[h, k - 1], recv_sem=s3_recv.at[h, k - 1],
                device_id=(2 * to + core, b), device_id_type=MESH,
            )
            cp.start()
            third[h, k] = cp

    features(0)
    features(2)
    group_sum(0)

    def feat_out(s, carry):
        cbuf[s] = jnp.concatenate(
            [cf[h, pl.ds(s * cs, opix), :] for h in range(2)], axis=1
        ).astype(BF16)
        return carry

    lax.fori_loop(0, owned, feat_out, 0)
    feat_copy = local_copy(cbuf, feat_ref, loc_sem.at[5])
    group_sum(1)
    sums = []
    for h in range(2):
        at = bounds[h]
        total = own3[z, :, at]
        for k in range(1, nz):
            third[h, k].wait_recv()
            total = total + r3[k - 1, :, at].astype(F32)[0:cw]
        sums.append(total * cfg["factor"])
    total = jnp.concatenate(sums, axis=1)
    sp_sum, tp_sum = total[:, :sp_lanes], total[:, sp_lanes:]
    if rs % 128:
        sp_sum = pltpu.roll(sp_sum, lax.rem(sp_lanes - lax.rem(b * rs, 128), sp_lanes), 1)
    if rt % 128:
        tp_sum = pltpu.roll(tp_sum, lax.rem(128 - lax.rem(b * rt, 128), 128), 1)
    sp_ref[...] = sp_sum[:, :rs]
    tp_ref[...] = tp_sum[:, :rt]

    feat_copy.wait()
    for group in (gathers, relays, forwards, first, second, third):
        for cp in group.values():
            cp.wait_send()


def hand_out(feat_in, sp_in, tp_in, feat_out, sp_out, tp_out, feat_buf, sp_buf, tp_buf, sem):
    ways = (
        (feat_in, feat_buf, feat_out), (sp_in, sp_buf, sp_out), (tp_in, tp_buf, tp_out)
    )
    loads = [pltpu.make_async_copy(w[0], w[1], sem.at[0, n]) for n, w in enumerate(ways)]
    stores = [pltpu.make_async_copy(w[1], w[2], sem.at[1, n]) for n, w in enumerate(ways)]
    for cp in loads:
        cp.start()
    for load, store in zip(loads, stores):
        load.wait()
        store.start()
    for cp in stores:
        cp.wait()


def per_device(tiles, cotangent, halo_flags, send_plan, spatial_weight, temporal_weight):
    nd, nb = lax.axis_size("dp"), lax.axis_size("bal")
    owned, cells, C = tiles.shape
    opix = cotangent.shape[1]
    rs, rt = spatial_weight.shape[0], temporal_weight.shape[0]
    S = up(owned, 8)
    nt = max(-(-(rs * (n + 1)) // 128) - rs * n // 128 for n in range(nb))
    sp_lanes = nt * 128
    nl = sp_lanes + 128
    cw = C // nd
    cwp = up(cw, 16)
    nz = nd // 2
    half = C // 2
    n_parts = 4
    parts = [owned // n_parts + (n < owned % n_parts) for n in range(n_parts)]
    cfg = dict(
        nd=nd, nb=nb, owned=owned, C=C, S=S, rs=rs, rt=rt, nt=nt, nl=nl, cw=cw, cwp=cwp,
        parts=parts, factor=1.0 / math.sqrt(nd * nb * WORK_TILES),
    )
    M = FR * TR * TC * S
    K = TO * TR * TC * S
    vm = pltpu.VMEM
    dma = pltpu.SemaphoreType.DMA
    hbm = pl.BlockSpec(memory_space=pltpu.HBM)
    vspec = pl.BlockSpec(memory_space=pltpu.VMEM)
    scratch = [
        vm((owned, opix, C), BF16),
        vm((3, owned), jnp.int32),
        pltpu.SMEM(send_plan.shape, jnp.int32),
        vm((8, 128), F32),
        vm((owned, cells, C), BF16),
        vm((2, S * (cells + 1), 128), F32),
        vm((2, S * (opix + 1), 128), F32),
        vm((M, 9 * C), BF16),
        vm((K, C), BF16),
        vm((9 * C, C), BF16),
        vm((2 * C, C), BF16),
        vm((M, C), BF16),
        vm((8, 128), F32),
        vm((C, M), BF16),
        vm((C, K), BF16),
        vm((S, 128), F32),
        vm((3, S, 128), F32),
        vm((nb, half, nl), F32),
        vm((nb, half, nl), BF16),
        vm((nb, half, nl), BF16),
        vm((nb - 1, half, nl), BF16),
        vm((nb - 1, half, nl), BF16),
        vm((nz, cw, nl), F32),
        vm((nz, cwp, nl), BF16),
        vm((nz - 1, cwp, nl), BF16),
        dma((n_parts,)),
        dma((6,)),
        dma((2, nb - 1)), dma((2, nb - 1)), dma((2, nb - 1)), dma((2, nb - 1)),
        dma((2, 2, nb - 1)), dma((2, 2, nb - 1)),
        dma((2, nb)), dma((2, nb)),
        dma((2, nb - 1)), dma((2, nb - 1)),
        dma((2, nz - 1)), dma((2, nz - 1)),
    ]
    shapes = (
        jax.ShapeDtypeStruct((owned, opix, C), BF16),
        jax.ShapeDtypeStruct((cw, rs), F32),
        jax.ShapeDtypeStruct((cw, rt), F32),
    )
    results = pl.pallas_call(
        functools.partial(kernel, cfg),
        out_shape=shapes,
        in_specs=[hbm] * 6,
        out_specs=(hbm, vspec, vspec),
        scratch_shapes=scratch,
        compiler_params=pltpu.CompilerParams(
            collective_id=0, has_side_effects=True, vmem_limit_bytes=VMEM_LIMIT
        ),
    )(tiles, cotangent, halo_flags.T, send_plan, spatial_weight, temporal_weight)
    features, sp, tp = pl.pallas_call(
        hand_out,
        out_shape=shapes,
        in_specs=[hbm] * 3,
        out_specs=(hbm, hbm, hbm),
        scratch_shapes=[vm(x.shape, x.dtype) for x in shapes] + [dma((2, 3))],
        compiler_params=pltpu.CompilerParams(vmem_limit_bytes=VMEM_LIMIT),
    )(*results)
    return (features, sp.T, tp.T)


def solution(mesh):
    in_specs = (
        P(("dp", "bal"), None, None),
        P(("dp", "bal"), None, None),
        P(("dp", "bal"), None),
        P(("dp", "bal"), None, None),
        P("bal", None),
        P("bal", None),
    )
    out_specs = (P(("dp", "bal"), None, None), P("bal", "dp"), P("bal", "dp"))
    return jax.shard_map(
        per_device, mesh=mesh, in_specs=in_specs, out_specs=out_specs, check_vma=False
    )
```

```python
import functools
import math

import jax
import jax.numpy as jnp
from jax import lax
from jax.experimental import pallas as pl
from jax.experimental.pallas import tpu as pltpu
from jax.sharding import PartitionSpec as P

FR, H, W = 6, 5, 9
TR, TC, TO = 2, 4, 4
WORK_TILES = 12
F32, BF16 = jnp.float32, jnp.bfloat16
MESH = pl.DeviceIdType.MESH
VMEM_LIMIT = 64 * 1024 * 1024 - 65536


def up(value, step):
    return (value + step - 1) // step * step


def kernel(
    cfg,
    tiles_ref, cot_ref, flags_ref, plan_ref, wsp_ref, wtp_ref,
    feat_ref, sp_ref, tp_ref,
    cbuf, fbuf, pbuf, ftmp, tbuf, xf, cf, patches, cotp, wsp, wtp, act, dact, grad_t, cot_t, live, masks,
    own, s1, r1, s2, r2, own3, s3, r3,
    tile_sem, loc_sem, ag_send, ag_recv, zr_send, zr_recv, fw_send, fw_recv,
    s1_send, s1_recv, s2_send, s2_recv, s3_send, s3_recv,
):
    nd, nb, owned, C = cfg["nd"], cfg["nb"], cfg["owned"], cfg["C"]
    S, rs, rt, nt, nl = cfg["S"], cfg["rs"], cfg["rt"], cfg["nt"], cfg["nl"]
    cw, cwp, parts = cfg["cw"], cfg["cwp"], cfg["parts"]
    nz = nd // 2
    cells, opix = FR * H * W, TO * TR * TC
    ts, cs = cells + 1, opix + 1
    FS = TR * TC * S
    half = C // 2

    d = lax.axis_index("dp")
    b = lax.axis_index("bal")
    core = lax.rem(d, 2)
    z = d // 2
    mate = d + 1 - 2 * core

    def bal_peer(k):
        return lax.rem(b + k, nb)

    def z_peer(k):
        return lax.rem(z + k, nz)

    def local_copy(src, dst, sem):
        cp = pltpu.make_async_copy(src, dst, sem)
        cp.start()
        return cp

    barrier = pltpu.get_barrier_semaphore()
    pl.semaphore_signal(barrier, inc=1, device_id=(mate, b), device_id_type=MESH)
    for k in range(1, nb):
        pl.semaphore_signal(barrier, inc=1, device_id=(d, bal_peer(k)), device_id_type=MESH)
    for k in range(1, nz):
        pl.semaphore_signal(
            barrier, inc=1, device_id=(2 * z_peer(k) + core, b), device_id_type=MESH
        )

    my_sp = pl.ds(pl.multiple_of(b * rs, 16), rs)
    my_tp = pl.ds(pl.multiple_of(b * rt, 16), rt)
    local = [
        local_copy(wsp_ref, wsp.at[my_sp], loc_sem.at[0]),
        local_copy(wtp_ref, wtp.at[my_tp], loc_sem.at[1]),
    ]
    small_copies = [
        local_copy(flags_ref, fbuf, loc_sem.at[2]),
        local_copy(plan_ref, pbuf, loc_sem.at[3]),
        local_copy(cot_ref, cbuf, loc_sem.at[4]),
    ]
    tile_copies = []
    lo = 0
    for n, count in enumerate(parts):
        part = pl.ds(lo, count)
        cp = local_copy(tiles_ref.at[part], tbuf.at[part], tile_sem.at[n])
        tile_copies.append((cp, lo, count))
        lo += count
    if S > owned:
        for h in range(2):
            cf[h, owned * cs : S * cs, :] = jnp.zeros(((S - owned) * cs, 128), F32)
            xf[h, owned * ts : S * ts, :] = jnp.zeros(((S - owned) * ts, 128), F32)

    for cp in local:
        cp.wait()
    pl.semaphore_wait(barrier, nb + nz - 1)

    lanes = pl.ds(pl.multiple_of(core * half, 128), half)
    zpar = lax.rem(z, 2)
    zmate = 2 * (z + 1 - 2 * zpar) + core
    weights = []
    for src, dst, size in ((wsp_ref, wsp, rs), (wtp_ref, wtp, rt)):
        units = size // 16
        fetch = units if nz % 2 else max((units + 1) // 2, round(0.6 * units))
        weights.append((src, dst, size, fetch * 16, (units - fetch) * 16))

    def rows_at(start, count):
        return pl.ds(pl.multiple_of(start, 16), count)

    gathers, relays, forwards = {}, {}, {}
    for k in range(1, nb):
        for n, (src, dst, size, fetch, rest) in enumerate(weights):
            cp = pltpu.make_async_remote_copy(
                src_ref=dst.at[rows_at(b * size + zpar * rest, fetch), lanes],
                dst_ref=dst.at[rows_at(b * size + zpar * rest, fetch), lanes],
                send_sem=ag_send.at[n, k - 1],
                recv_sem=ag_recv.at[n, k - 1],
                device_id=(d, bal_peer(k)),
                device_id_type=MESH,
            )
            cp.start()
            gathers[n, k] = cp

    def push(ref, rows, to, send, recv):
        cp = pltpu.make_async_remote_copy(
            src_ref=ref.at[rows, lanes], dst_ref=ref.at[rows, lanes],
            send_sem=send, recv_sem=recv, device_id=(to, b), device_id_type=MESH,
        )
        cp.start()
        return cp

    def relay(k):
        origin = lax.rem(b + nb - k, nb)
        for n, (src, dst, size, fetch, rest) in enumerate(weights):
            gathers[n, k].wait_recv()
            if rest:
                relays[n, k] = push(
                    dst, rows_at(origin * size + zpar * fetch, rest), zmate,
                    zr_send.at[n, k - 1], zr_recv.at[n, k - 1],
                )
            forwards[0, n, k] = push(
                dst, rows_at(origin * size + zpar * rest, fetch), mate,
                fw_send.at[0, n, k - 1], fw_recv.at[0, n, k - 1],
            )

    def relay_rest(k):
        origin = lax.rem(b + nb - k, nb)
        for n, (src, dst, size, fetch, rest) in enumerate(weights):
            if rest:
                relays[n, k].wait_recv()
                forwards[1, n, k] = push(
                    dst, rows_at(origin * size + (1 - zpar) * fetch, rest), mate,
                    fw_send.at[1, n, k - 1], fw_recv.at[1, n, k - 1],
                )

    for cp in small_copies:
        cp.wait()
    slot = lax.broadcasted_iota(jnp.int32, (S, 128), 0)
    lane = lax.broadcasted_iota(jnp.int32, (S, 128), 1)
    ftmp[...] = jnp.zeros_like(ftmp)
    ftmp[0:3, 0:owned] = (fbuf[...] > 0).astype(F32)
    for n in range(3):
        row = jnp.broadcast_to(ftmp[n : n + 1, :], (S, 128))
        column = jnp.sum(jnp.where(slot == lane, row, 0.0), axis=1, keepdims=True)
        masks[n] = jnp.broadcast_to(column, (S, 128))
    found = jnp.zeros((S, 128), F32)
    for w in range(pbuf.shape[1]):
        for q in range(pbuf.shape[2]):
            found = jnp.maximum(found, jnp.where(slot == pbuf[0, w, q], 1.0, 0.0))
    live[...] = found

    def cot_in(s, carry):
        v = cbuf[s].astype(F32)
        for h in range(2):
            cf[h, pl.ds(s * cs, opix), :] = v[:, h * 128 : (h + 1) * 128]
        return carry

    lax.fori_loop(0, owned, cot_in, 0)
    lv = live[...]

    def cot_rows(p, carry):
        for h in range(2):
            pair = [
                cf[h, pl.ds(2 * p + n, S, stride=cs), :] * lv for n in range(2)
            ]
            cotp[pl.ds(pl.multiple_of(p * 2 * S, 16), 2 * S), h * 128 : (h + 1) * 128] = (
                jnp.concatenate(pair, axis=0).astype(BF16)
            )
        return carry

    lax.fori_loop(0, opix // 2, cot_rows, 0)

    def split_rows(v):
        cores = [
            jnp.concatenate(
                [v[(2 * n + q) * cw : (2 * n + q + 1) * cw] for n in range(nz)], axis=0
            )
            for q in range(2)
        ]
        return cores

    def store_split(ref, v, lo, width):
        cores = split_rows(v)
        for q in range(2):
            at = core if q == 1 else 0
            at = (1 - core) if q == 1 else core
            ref[pl.ds(pl.multiple_of(at * half, 128), half), lo : lo + width] = cores[
                q
            ].astype(BF16)

    for n in range(2):
        rows = n * 2 * FS
        store_split(cot_t, cotp[rows : rows + 2 * FS, :].astype(BF16 if cw % 16 == 0 else F32).T, rows, 2 * FS)

    def tile_in(s, carry):
        v = tbuf[s].astype(F32)
        for h in range(2):
            xf[h, pl.ds(s * ts, cells), :] = v[:, h * 128 : (h + 1) * 128]
        return carry

    for cp, lo, count in tile_copies:
        cp.wait()
        lax.fori_loop(lo, lo + count, tile_in, 0)

    top, left, past = masks[0], masks[1], masks[2]

    def patch_rows(f, carry):
        hist = jnp.where(f >= 2, jnp.ones_like(past), past)
        hist_top, hist_left = hist * top, hist * left
        hist_both = hist_top * left
        for r in range(H):
            uses = [(r - 2 * i, i) for i in range(TR) if 0 <= r - 2 * i < 3]
            mask = hist_top if r == 0 else hist
            mask_left = hist_both if r == 0 else hist_left
            for h in range(2):
                cols = [
                    xf[h, pl.ds(f * (H * W) + r * W + c, S, stride=ts), :]
                    * (mask_left if c == 0 else mask)
                    for c in range(W)
                ]
                for kx in range(3):
                    for jp in range(TC // 2):
                        c = 4 * jp + kx
                        v = jnp.concatenate([cols[c], cols[c + 2]], axis=0).astype(BF16)
                        for ky, i in uses:
                            row = pl.ds(
                                pl.multiple_of(f * FS + (i * TC + 2 * jp) * S, 16), 2 * S
                            )
                            at = (3 * ky + kx) * C + h * 128
                            patches[row, at : at + 128] = v
        return carry

    steps = max(nb - 1, 1)
    cuts = [FR * n // steps for n in range(steps + 1)]
    for n in range(steps):
        if n + 1 < nb:
            relay(n + 1)
        if n > 1:
            relay_rest(n - 1)
        if cuts[n + 1] > cuts[n]:
            lax.fori_loop(cuts[n], cuts[n + 1], patch_rows, 0)
    for k in range(max(steps - 1, 1), nb):
        relay_rest(k)
    for cp in forwards.values():
        cp.wait_recv()

    def chunk(n):
        rows = n * 2 * FS
        pre = jnp.dot(patches[rows : rows + 2 * FS, :], wsp[...], preferred_element_type=F32)
        sig = 1.0 / (1.0 + jnp.exp(-pre))
        act[rows : rows + 2 * FS, :] = (pre * sig).astype(BF16)
        ga = None
        nt_dims = (((1,), (1,)), ((), ()))
        if n > 0:
            lo = (n - 1) * 2 * FS
            ga = lax.dot_general(
                cotp[lo : lo + 2 * FS, :], wtp[0:C, :], nt_dims, preferred_element_type=F32
            )
        if n < 2:
            g = lax.dot_general(
                cotp[rows : rows + 2 * FS, :], wtp[C : 2 * C, :], nt_dims,
                preferred_element_type=F32,
            )
            ga = g if ga is None else ga + g
        gp = ga * (sig * (1.0 + pre * (1.0 - sig)))
        store_split(grad_t, (gp.astype(BF16) if cw % 16 == 0 else gp).T, rows, 2 * FS)

    for n in range(3):
        chunk(n)

    sp_lanes = nt * 128
    cut = (nt + 2) // 2
    spans = [(0, cut), (cut, nt)]
    bounds = [pl.ds(0, cut * 128), pl.ds(cut * 128, nl - cut * 128)]

    def section(h, k):
        to = bal_peer(k)
        lo, hi = spans[h]
        if hi > lo:
            sp_at = pl.multiple_of((to * rs) // 128 * 128 + lo * 128, 128)
            g = jnp.dot(
                grad_t[...], patches[:, pl.ds(sp_at, (hi - lo) * 128)],
                preferred_element_type=F32,
            )
            own[k - 1, :, lo * 128 : hi * 128] = g[0:half]
            s1[k - 1, :, lo * 128 : hi * 128] = g[half:].astype(BF16)
        if h == 1:
            tp_at = (to * rt) // 128 * 128
            tap = tp_at // C
            at = pl.multiple_of(tp_at - tap * C, 128)
            rows = pl.ds(pl.multiple_of((1 - tap) * 2 * FS, 16), TO * FS)
            g = jnp.dot(cot_t[...], act[rows, pl.ds(at, 128)], preferred_element_type=F32)
            own[k - 1, :, sp_lanes:] = g[0:half]
            s1[k - 1, :, sp_lanes:] = g[half:].astype(BF16)
        cp = pltpu.make_async_remote_copy(
            src_ref=s1.at[k - 1, :, bounds[h]], dst_ref=r1.at[k - 1, :, bounds[h]],
            send_sem=s1_send.at[h, k - 1], recv_sem=s1_recv.at[h, k - 1],
            device_id=(mate, b), device_id_type=MESH,
        )
        cp.start()
        first[h, k] = cp

    first, second, third = {}, {}, {}

    def pass_on(h, k):
        first[h, k].wait_recv()
        at = bounds[h]
        total = own[k - 1, :, at] + r1[k - 1, :, at].astype(F32)
        if k == nb:
            own[k - 1, :, at] = total
            return
        s2[k - 1, :, at] = total.astype(BF16)
        cp = pltpu.make_async_remote_copy(
            src_ref=s2.at[k - 1, :, at], dst_ref=r2.at[k - 1, :, at],
            send_sem=s2_send.at[h, k - 1], recv_sem=s2_recv.at[h, k - 1],
            device_id=(d, bal_peer(k)), device_id_type=MESH,
        )
        cp.start()
        second[h, k] = cp

    order = [(h, k) for h in range(2) for k in range(1, nb + 1)]
    lag = min(3, nb)
    for n, unit in enumerate(order):
        section(*unit)
        if n >= lag:
            pass_on(*order[n - lag])
    for unit in order[-lag:]:
        pass_on(*unit)

    def features(t0):
        rows = t0 * FS
        feat = jnp.dot(
            act[rows + 2 * FS : rows + 4 * FS, :], wtp[0:C, :], preferred_element_type=F32
        ) + jnp.dot(act[rows : rows + 2 * FS, :], wtp[C : 2 * C, :], preferred_element_type=F32)
        for p in range(2 * TR * TC):
            for h in range(2):
                v = feat[p * S : (p + 1) * S, h * 128 : (h + 1) * 128]
                cf[h, pl.ds(t0 * TR * TC + p, S, stride=cs), :] = v * lv

    def group_sum(h):
        at = bounds[h]
        total = own[nb - 1, :, at]
        for k in range(1, nb):
            second[h, k].wait_recv()
            total = total + r2[k - 1, :, at].astype(F32)
        for n in range(nz):
            part = total[n * cw : (n + 1) * cw]
            own3[n, :, at] = part
            if cwp > cw:
                part = jnp.concatenate(
                    [part, jnp.zeros((cwp - cw, part.shape[1]), F32)], axis=0
                )
            s3[n, :, at] = part.astype(BF16)
        for k in range(1, nz):
            to = z_peer(k)
            cp = pltpu.make_async_remote_copy(
                src_ref=s3.at[to, :, at], dst_ref=r3.at[k - 1, :, at],
                send_sem=s3_send.at[h, k - 1], recv_sem=s3_recv.at[h, k - 1],
                device_id=(2 * to + core, b), device_id_type=MESH,
            )
            cp.start()
            third[h, k] = cp

    features(0)
    group_sum(0)
    features(2)

    def feat_out(s, carry):
        cbuf[s] = jnp.concatenate(
            [cf[h, pl.ds(s * cs, opix), :] for h in range(2)], axis=1
        ).astype(BF16)
        return carry

    lax.fori_loop(0, owned, feat_out, 0)
    feat_copy = local_copy(cbuf, feat_ref, loc_sem.at[5])
    group_sum(1)
    sums = []
    for h in range(2):
        at = bounds[h]
        total = own3[z, :, at]
        for k in range(1, nz):
            third[h, k].wait_recv()
            total = total + r3[k - 1, :, at].astype(F32)[0:cw]
        sums.append(total * cfg["factor"])
    total = jnp.concatenate(sums, axis=1)
    sp_sum, tp_sum = total[:, :sp_lanes], total[:, sp_lanes:]
    if rs % 128:
        sp_sum = pltpu.roll(sp_sum, lax.rem(sp_lanes - lax.rem(b * rs, 128), sp_lanes), 1)
    if rt % 128:
        tp_sum = pltpu.roll(tp_sum, lax.rem(128 - lax.rem(b * rt, 128), 128), 1)
    sp_ref[...] = sp_sum[:, :rs]
    tp_ref[...] = tp_sum[:, :rt]

    feat_copy.wait()
    for group in (gathers, relays, forwards, first, second, third):
        for cp in group.values():
            cp.wait_send()


def hand_out(feat_in, sp_in, tp_in, feat_out, sp_out, tp_out, feat_buf, sp_buf, tp_buf, sem):
    ways = (
        (feat_in, feat_buf, feat_out), (sp_in, sp_buf, sp_out), (tp_in, tp_buf, tp_out)
    )
    loads = [pltpu.make_async_copy(w[0], w[1], sem.at[0, n]) for n, w in enumerate(ways)]
    stores = [pltpu.make_async_copy(w[1], w[2], sem.at[1, n]) for n, w in enumerate(ways)]
    for cp in loads:
        cp.start()
    for load, store in zip(loads, stores):
        load.wait()
        store.start()
    for cp in stores:
        cp.wait()


def per_device(tiles, cotangent, halo_flags, send_plan, spatial_weight, temporal_weight):
    nd, nb = lax.axis_size("dp"), lax.axis_size("bal")
    owned, cells, C = tiles.shape
    opix = cotangent.shape[1]
    rs, rt = spatial_weight.shape[0], temporal_weight.shape[0]
    S = up(owned, 8)
    nt = max(-(-(rs * (n + 1)) // 128) - rs * n // 128 for n in range(nb))
    sp_lanes = nt * 128
    nl = sp_lanes + 128
    cw = C // nd
    cwp = up(cw, 16)
    nz = nd // 2
    half = C // 2
    n_parts = 4
    parts = [owned // n_parts + (n < owned % n_parts) for n in range(n_parts)]
    cfg = dict(
        nd=nd, nb=nb, owned=owned, C=C, S=S, rs=rs, rt=rt, nt=nt, nl=nl, cw=cw, cwp=cwp,
        parts=parts, factor=1.0 / math.sqrt(nd * nb * WORK_TILES),
    )
    M = FR * TR * TC * S
    K = TO * TR * TC * S
    vm = pltpu.VMEM
    dma = pltpu.SemaphoreType.DMA
    hbm = pl.BlockSpec(memory_space=pltpu.HBM)
    vspec = pl.BlockSpec(memory_space=pltpu.VMEM)
    scratch = [
        vm((owned, opix, C), BF16),
        vm((3, owned), jnp.int32),
        pltpu.SMEM(send_plan.shape, jnp.int32),
        vm((8, 128), F32),
        vm((owned, cells, C), BF16),
        vm((2, S * (cells + 1), 128), F32),
        vm((2, S * (opix + 1), 128), F32),
        vm((M, 9 * C), BF16),
        vm((K, C), BF16),
        vm((9 * C, C), BF16),
        vm((2 * C, C), BF16),
        vm((M, C), BF16),
        vm((8, 128), F32),
        vm((C, M), BF16),
        vm((C, K), BF16),
        vm((S, 128), F32),
        vm((3, S, 128), F32),
        vm((nb, half, nl), F32),
        vm((nb, half, nl), BF16),
        vm((nb, half, nl), BF16),
        vm((nb - 1, half, nl), BF16),
        vm((nb - 1, half, nl), BF16),
        vm((nz, cw, nl), F32),
        vm((nz, cwp, nl), BF16),
        vm((nz - 1, cwp, nl), BF16),
        dma((n_parts,)),
        dma((6,)),
        dma((2, nb - 1)), dma((2, nb - 1)), dma((2, nb - 1)), dma((2, nb - 1)),
        dma((2, 2, nb - 1)), dma((2, 2, nb - 1)),
        dma((2, nb)), dma((2, nb)),
        dma((2, nb - 1)), dma((2, nb - 1)),
        dma((2, nz - 1)), dma((2, nz - 1)),
    ]
    shapes = (
        jax.ShapeDtypeStruct((owned, opix, C), BF16),
        jax.ShapeDtypeStruct((cw, rs), F32),
        jax.ShapeDtypeStruct((cw, rt), F32),
    )
    results = pl.pallas_call(
        functools.partial(kernel, cfg),
        out_shape=shapes,
        in_specs=[hbm] * 6,
        out_specs=(hbm, vspec, vspec),
        scratch_shapes=scratch,
        compiler_params=pltpu.CompilerParams(
            collective_id=0, has_side_effects=True, vmem_limit_bytes=VMEM_LIMIT
        ),
    )(tiles, cotangent, halo_flags.T, send_plan, spatial_weight, temporal_weight)
    features, sp, tp = pl.pallas_call(
        hand_out,
        out_shape=shapes,
        in_specs=[hbm] * 3,
        out_specs=(hbm, hbm, hbm),
        scratch_shapes=[vm(x.shape, x.dtype) for x in shapes] + [dma((2, 3))],
        compiler_params=pltpu.CompilerParams(vmem_limit_bytes=VMEM_LIMIT),
    )(*results)
    return (features, sp.T, tp.T)


def solution(mesh):
    in_specs = (
        P(("dp", "bal"), None, None),
        P(("dp", "bal"), None, None),
        P(("dp", "bal"), None),
        P(("dp", "bal"), None, None),
        P("bal", None),
        P("bal", None),
    )
    out_specs = (P(("dp", "bal"), None, None), P("bal", "dp"), P("bal", "dp"))
    return jax.shard_map(
        per_device, mesh=mesh, in_specs=in_specs, out_specs=out_specs, check_vma=False
    )
```
